32 devices in a mesh: sec: 2 (over x), lat: 4 (over z), lon: 4 (over y, core).
Axes of the slice: x: 2, y: 2, z: 4, core: 2. Of those that a mesh axis runs over, the one named last changes fastest.
Arguments:
- spectra: float32 [36, 36, 32, 512], P('sec', None, 'lat', 'lon'), may hold values from 0 to 2
- currents: float32 [2, 8, 32, 512], P(None, 'sec', 'lat', 'lon'), may hold values from -3 to 3
- land_mask: int32 [32, 512], P('lat', 'lon'), may hold values 0 or 1
- diffusion: float32 [32, 512], P('lat', 'lon'), may hold values from 0.08 to 0.19
- courant: float32 [36], P('sec'), may hold values from 0.15 to 0.45
- stokes_weight: float32 [36], P('sec'), may hold values from 0.02 to 0.1
- stress_weight: float32 [36], P('sec'), may hold values from 0.02 to 0.1
Outputs:
- new_spectra: float32 [36, 36, 32, 512], P('sec', None, 'lat', 'lon')
- new_currents: float32 [2, 8, 32, 512], P(None, 'sec', 'lat', 'lon')
The draws below stay inside these ranges and needn't reach their ends.
Inputs may be any that keep to these rules, and one draw needn't show every extreme that they name: `land_mask`: 1 marks a sea column, 0 a land column.
All inputs are finite; a program needn't handle non-finite values. No bound on the sum of `land_mask` on one device may be relied on, other than what follows from the above.
Results may differ from the reference program's by a relative error of at most 0.0001.
Values sent between devices are 32-bit elements; how exact they have to be, the bound alone decides.
No kernel may reach another device: no remote copies, remote signals or barrier semaphores. Data moves between devices by JAX's collectives and lax.ppermute only.
A program may use at most 128 MiB of HBM per device.

```python
import math
import jax
import jax.numpy as jnp
from jax import lax

FREQS = 36
DIRS = 36
ITERS = 4
LEVELS = 8
NLAT = 32
NLON = 512


def touch_ends(values, rng, low, largest):
    index_at = [jax.random.randint(jax.random.fold_in(rng, axis), (), 0, length) for axis, length in enumerate(values.shape)]
    longest = values.shape.index(max(values.shape))
    beside = index_at[:longest] + [(index_at[longest] + 1) % values.shape[longest]] + index_at[longest + 1:]
    return values.at[tuple(index_at)].set(low).at[tuple(beside)].set(largest)


def steps_of(own_key, shape, cuts, smallest, top_value):
    loudness, own = 1.0, jax.random.fold_in(own_key, 6)
    for position, parts in cuts:
        steps = jnp.exp(jax.random.uniform(jax.random.fold_in(own, position), (parts,), jnp.float32, smallest / len(cuts), top_value / len(cuts)))
        loudness = loudness * jnp.repeat(steps, shape[position] // parts).reshape([-1 if axis == position else 1 for axis in range(len(shape))])
    return loudness


def noise(key, dims, deviation, bound, pieces=(), dtype=jnp.bfloat16):
    result = jax.random.normal(key, dims, jnp.float32) * deviation
    if len(pieces) > 0:
        result = steps_of(key, dims, pieces, -0.22, 0.18) * result
    return jnp.clip(result, min=-bound, max=bound).astype(dtype)


def setup_inputs(seed: int = 0) -> dict:
    key_list = jax.random.split(jax.random.key(seed), 8)
    spectra = jnp.clip(2.0 * jax.random.uniform(key_list[0], (FREQS, DIRS, NLAT, NLON), jnp.float32) ** steps_of(key_list[0], (FREQS, DIRS, NLAT, NLON), ((0, 2), (2, 4), (3, 4)), -0.2, 0.2), 0.0, 2.0)
    currents = noise(key_list[1], (2, LEVELS, NLAT, NLON), 1.0, 3.0, ((1, 2), (2, 4), (3, 4)), jnp.float32)
    land_mask = touch_ends((jax.random.randint(key_list[2], (NLAT, NLON), 0, 4) < 3).astype(jnp.int32), jax.random.fold_in(key_list[2], 1), 0, 1)
    diffusion = jnp.clip(0.08 + 0.11 * jax.random.uniform(key_list[3], (NLAT, NLON), jnp.float32) ** steps_of(key_list[3], (NLAT, NLON), ((0, 4), (1, 4)), -0.2, 0.2), 0.08, 0.19)
    courant = jnp.clip(0.15 + 0.29999998 * jax.random.uniform(key_list[4], (FREQS,), jnp.float32) ** steps_of(key_list[4], (FREQS,), ((0, 2),), -0.2, 0.2), 0.15, 0.45)
    stokes_weight = jnp.clip(jnp.exp(math.log(0.1) - 1.609438 * jax.random.uniform(key_list[5], (FREQS,), jnp.float32) ** steps_of(key_list[5], (FREQS,), ((0, 2),), -0.2, 0.2)), 0.02, 0.1)
    stress_weight = jnp.clip(jnp.exp(math.log(0.1) - 1.609438 * jax.random.uniform(key_list[6], (FREQS,), jnp.float32) ** steps_of(key_list[6], (FREQS,), ((0, 2),), -0.2, 0.2)), 0.02, 0.1)
    return dict(spectra=spectra, currents=currents, land_mask=land_mask, diffusion=diffusion, courant=courant, stokes_weight=stokes_weight, stress_weight=stress_weight)


current_gain = 0.1
stress_gain = 0.5


def heading_tables(directions):
    heading = (jnp.arange(directions).astype(jnp.float32) + 0.5) * (2.0 * math.pi / directions)
    return jnp.cos(heading), jnp.sin(heading)


def wave_update(energy, west_cell, east_cell, south_cell, north_cell, speed, cosine_table, sine_table, surface, sea_cells):
    speed_x = (speed[:, None] * cosine_table[None])[:, :, None, None]
    speed_y = (speed[:, None] * sine_table[None])[:, :, None, None]
    step_x = jnp.maximum(speed_x, 0.0) * (energy - west_cell) + jnp.minimum(speed_x, 0.0) * (east_cell - energy)
    step_y = jnp.maximum(speed_y, 0.0) * (energy - south_cell) + jnp.minimum(speed_y, 0.0) * (north_cell - energy)
    advected = energy - step_x - step_y
    doppler = 1.0 + current_gain * (surface[0][None] * cosine_table[:, None, None] + surface[1][None] * sine_table[:, None, None])
    return sea_cells * (advected * doppler)


def coupling_weights(stokes_w, stress_w, cosine_table, sine_table):
    stacked = jnp.stack([stokes_w[:, None] * cosine_table[None], stokes_w[:, None] * sine_table[None],
                         stress_w[:, None] * cosine_table[None], stress_w[:, None] * sine_table[None]])
    return stacked.reshape(4, stokes_w.shape[0] * cosine_table.shape[0])


def vertical_rate(level):
    return 0.04 + 0.0125 * ((7 * level) % 5).astype(jnp.float32)


def coriolis_rate(row_index, total_rows):
    return 0.05 + 0.1 * (row_index.astype(jnp.float32) + 0.5) / total_rows


def ocean_step(extended, column_data, first_level, first_row, total_levels, total_rows):
    center = extended[:, 1:-1, 1:-1, 1:-1]
    laplace = (extended[:, 1:-1, 2:, 1:-1] + extended[:, 1:-1, :-2, 1:-1]
               + extended[:, 1:-1, 1:-1, 2:] + extended[:, 1:-1, 1:-1, :-2] - 4.0 * center)
    level_above = extended[:, :-2, 1:-1, 1:-1]
    level_below = extended[:, 2:, 1:-1, 1:-1]
    level = first_level + 1 + jnp.arange(center.shape[1])
    has_up = (level > 0)[:, None, None]
    has_down = (level < total_levels - 1)[:, None, None]
    mixing = vertical_rate(level)[:, None, None]
    vertical = mixing * (jnp.where(has_up, level_above - center, 0.0) + jnp.where(has_down, level_below - center, 0.0))
    stokes_decay = (1.0 / (1.0 + level.astype(jnp.float32)))[:, None, None]
    top_gain = jnp.where(level == 0, stress_gain, 0.0)[:, None, None]
    row_index = first_row + 1 + jnp.arange(center.shape[2])
    coriolis = coriolis_rate(row_index, total_rows)[:, None]
    sea_cells = column_data[0]
    kappa = column_data[1]
    zonal = center[0]
    meridional = center[1]
    zonal_new = sea_cells * (zonal + kappa * laplace[0] + vertical[0]
                             + coriolis * (meridional + stokes_decay * column_data[3]) + top_gain * column_data[4])
    meridional_new = sea_cells * (meridional + kappa * laplace[1] + vertical[1]
                                  - coriolis * (zonal + stokes_decay * column_data[2]) + top_gain * column_data[5])
    return jnp.stack([zonal_new, meridional_new])


def reference(spectra, currents, land_mask, diffusion, courant, stokes_weight, stress_weight):
    sea_cells = land_mask.astype(jnp.float32)
    cosine_table, sine_table = heading_tables(DIRS)
    surface = currents[:, 0]

    def per_freq(summed, inputs):
        energy, speed, stokes_w, stress_w = inputs
        energy = energy[None]
        west_cell = jnp.roll(energy, 1, axis=3)
        east_cell = jnp.roll(energy, -1, axis=3)
        zero_row = jnp.zeros_like(energy[:, :, :1])
        south_cell = jnp.concatenate([zero_row, energy[:, :, :-1]], axis=2)
        north_cell = jnp.concatenate([energy[:, :, 1:], zero_row], axis=2)
        updated = wave_update(energy, west_cell, east_cell, south_cell, north_cell, speed[None],
                              cosine_table, sine_table, surface, sea_cells)
        weights = coupling_weights(stokes_w[None], stress_w[None], cosine_table, sine_table)
        summed = summed + jnp.dot(weights, updated.reshape(DIRS, NLAT * NLON),
                                  precision=lax.Precision.HIGHEST, preferred_element_type=jnp.float32)
        return summed, updated[0]

    start = jnp.zeros((4, NLAT * NLON), jnp.float32)
    summed, new_spectra = lax.scan(per_freq, start, (spectra, courant, stokes_weight, stress_weight))
    coupling = summed.reshape(4, NLAT, NLON)
    column_data = jnp.concatenate([sea_cells[None], diffusion[None], coupling], axis=0)
    fields = currents * sea_cells
    for iteration in range(ITERS):
        padded = jnp.pad(fields, ((0, 0), (1, 1), (1, 1), (0, 0)))
        padded = jnp.concatenate([padded[..., -1:], padded, padded[..., :1]], axis=3)
        fields = ocean_step(padded, column_data, -1, -1, LEVELS, NLAT)
    return new_spectra, fields
```

```python
import functools
import math

import jax
import jax.numpy as jnp
import numpy as np
from jax import lax
from jax.experimental import pallas as pl
from jax.experimental.pallas import tpu as pltpu
from jax.sharding import PartitionSpec as P

ITERS = 4
ROWS = 8
LANES = 128
HALO = 4
MOMENTS = 5
SUMS = 2 * MOMENTS
FLUX_COLS = 3
current_gain = 0.1
stress_gain = 0.5

VMEM = pl.BlockSpec(memory_space=pltpu.VMEM)
SMEM = pl.BlockSpec(memory_space=pltpu.SMEM)
ANY = pl.BlockSpec(memory_space=pl.ANY)
F32 = jnp.float32


def lanes():
    return lax.broadcasted_iota(jnp.int32, (ROWS, LANES), 1)


def rows():
    return lax.broadcasted_iota(jnp.int32, (ROWS, LANES), 0)


def lane_roll(tile, shift):
    if isinstance(shift, int):
        shift %= LANES
        if shift == 0:
            return tile
    return pltpu.roll(tile, shift, 1)


def row_roll(tile, shift):
    shift %= ROWS
    return tile if shift == 0 else pltpu.roll(tile, shift, 0)


def spread(ref, row):
    return jnp.broadcast_to(ref[pl.ds(row, 1), :], (ROWS, LANES))


def put(ref, index, tile):
    ref[pl.ds(index * ROWS, ROWS), :] = tile


def take(ref, index):
    return ref[pl.ds(index * ROWS, ROWS), :]


def coupled(sums, zonal, meridional, sea):
    result = []
    for w in range(2):
        c, s, cc, cs, ss = sums[w * MOMENTS : (w + 1) * MOMENTS]
        result.append(sea * (c + current_gain * (zonal * cc + meridional * cs)))
        result.append(sea * (s + current_gain * (zonal * cs + meridional * ss)))
    return result


class Sizes:
    def __init__(self, freqs, directions, levels):
        self.freqs = freqs
        self.directions = directions
        self.levels = levels
        self.quarter = directions // 4
        self.fields = 2 * 2 * levels
        self.half = directions // 2
        self.per_tile = LANES // self.half
        self.col_tiles = -(-freqs // self.per_tile)
        self.edge_rows = freqs * directions // 2
        self.sec_sums = self.fields // 2
        self.sec_cols = self.sec_sums + SUMS
        self.sec_rows = self.sec_cols + 1
        self.sec_tiles = self.sec_rows + -(-2 * SUMS // ROWS)
        self.lon_coup = HALO * (self.fields + 2)
        self.lon_flux = self.lon_coup + 4 * HALO
        self.lon_rows = self.lon_flux + SUMS
        self.arrays = self.fields + 2 + 4
        self.pairs = self.arrays // 2
        self.flux_tiles = -(-SUMS // ROWS)
        self.lat_pairs = 0
        self.lat_flux = self.lat_pairs + self.pairs
        self.lat_edges = self.lat_flux + self.flux_tiles
        self.lat_tiles = self.lat_edges + 1
        self.coef_tiles = -(-freqs // ROWS)
        assert self.lon_rows + SUMS * FLUX_COLS <= LANES
        assert (self.pairs + self.flux_tiles) * 2 * HALO <= LANES

    def headings(self, i):
        q = self.quarter
        return (i, 2 * q - 1 - i, 2 * q + i, 4 * q - 1 - i)


def chunks(z):
    q = z.quarter
    group = 3 if q % 3 == 0 else 1
    result = []
    for lo in range(0, q, group):
        hi = lo + group
        result.append((lo, hi, [pl.ds(start, group) for start in (lo, 2 * q - hi, 2 * q + lo, 4 * q - hi)]))
    return result


def sums_kernel(z, x, cur_in, mask_in, diffusion_in, courant_in, stokes_in, stress_in, table_in, buf, pay, first_rows, second_rows, ecol, wcol, local, coef, cur, mask, courant, stokes, stress, table, acc, sems, small_sems):
    q, nf = z.quarter, z.freqs
    pairs = ((cur_in, cur), (mask_in, mask), (diffusion_in, local.at[pl.ds(ROWS, ROWS)]), (courant_in, courant), (stokes_in, stokes), (stress_in, stress), (table_in, table))
    small = [pltpu.make_async_copy(source, target, small_sems.at[k]) for k, (source, target) in enumerate(pairs)]
    for copy in small:
        copy.start()
    copies = []
    for g, (_, _, spans) in enumerate(chunks(z)):
        for j, span in enumerate(spans):
            copies.append(pltpu.make_async_copy(x.at[:, span], buf.at[:, span], sems.at[4 * g + j]))
    for copy in copies:
        copy.start()

    lane, row = lanes(), rows()
    zero = jnp.zeros((ROWS, LANES), F32)
    for k in range(5 * SUMS):
        acc[k] = zero
    for t in range(z.col_tiles):
        put(ecol, t, zero)
        put(wcol, t, zero)
    for copy in small:
        copy.wait()
    sea = mask[...].astype(F32)
    put(local, 0, sea)
    for comp in range(2):
        for level in range(z.levels):
            put(pay, comp * z.levels + level, cur[comp, level] * sea)
    for f in range(nf):
        coef[pl.ds(f, 1), :] = jnp.full((1, LANES), courant[f], F32)

    def body(i, _):
        c, s = table[0, i], table[1, i]
        heading = z.headings(i)
        total = [[zero] * 4 for _ in range(4)]
        east, west = [zero] * z.col_tiles, [zero] * z.col_tiles
        for f in range(nf):
            t = f // z.per_tile
            cg = courant[f]
            factors = (stokes[f], stokes[f] * cg, stress[f], stress[f] * cg)
            for j in range(4):
                energy = buf[f, heading[j]]
                for k in range(4):
                    total[k][j] = total[k][j] + factors[k] * energy
                at = f % z.per_tile * z.half + (0 if j in (0, 1) else 1)
                if j in (0, 3):
                    east[t] = jnp.where(lane == at, lane_roll(energy, at - (LANES - 1)), east[t])
                else:
                    west[t] = jnp.where(lane == at, lane_roll(energy, at), west[t])
        mine = lax.div(lax.rem(lane, z.half), 2) == i
        for ref, tiles in ((ecol, east), (wcol, west)):
            for t in range(z.col_tiles):
                put(ref, t, jnp.where(mine, lane_roll(tiles[t], 2 * i), take(ref, t)))
        cc, cs, ss = c * c, c * s, s * s
        for w in range(2):
            plain, fast = total[2 * w], total[2 * w + 1]
            both = c + s
            h = [plain[j] - both * fast[j] for j in range(4)]
            here, there = h[0] + h[3], h[1] + h[2]
            every = here + there
            values = [
                c * (here - there),
                s * ((h[0] + h[1]) - (h[2] + h[3])),
                cc * every,
                cs * ((h[0] - h[3]) + (h[2] - h[1])),
                ss * every,
            ]
            for a, b, size, signs in (
                (fast[0] + fast[3], fast[0] - fast[3], c, (1, 1, 1)),
                (fast[1] + fast[2], fast[1] - fast[2], c, (-1, 1, -1)),
            ):
                values += [signs[0] * size * c * a, signs[1] * size * s * b, size * cc * a, signs[2] * size * cs * b, size * ss * a]
            for a, b, size, signs in (
                (fast[0] + fast[1], fast[0] - fast[1], s, (1, 1, 1)),
                (fast[2] + fast[3], fast[3] - fast[2], s, (1, -1, -1)),
            ):
                values += [signs[0] * size * c * b, signs[1] * size * s * a, size * cc * a, signs[2] * size * cs * b, size * ss * a]
            for kind in range(5):
                for m in range(MOMENTS):
                    at = kind * SUMS + w * MOMENTS + m
                    acc[at] = acc[at] + values[kind * MOMENTS + m]
        return 0

    for g, (lo, hi, _) in enumerate(chunks(z)):
        for copy in copies[4 * g : 4 * g + 4]:
            copy.wait()
        lax.fori_loop(lo, hi, body, 0)

    flat = buf.reshape(nf * z.directions * ROWS, LANES)
    odd = lax.rem(lax.axis_index("lat"), 2)
    north, south = ROWS - 1, z.half * ROWS
    for ref, start in ((first_rows, north + odd * (south - north)), (second_rows, south + odd * (north - south))):
        for f in range(nf):
            ref[pl.ds(f * z.half, z.half), :] = flat[pl.ds(f * z.directions * ROWS + start, z.half, stride=ROWS), :]

    cols = zero
    for k in range(SUMS):
        center, east, west, north, south = (acc[kind * SUMS + k] for kind in range(5))
        value = center + jnp.where(lane > 0, lane_roll(east, 1), 0.0) + jnp.where(lane < LANES - 1, lane_roll(west, -1), 0.0)
        value = value + jnp.where(row > 0, row_roll(north, 1), 0.0) + jnp.where(row < ROWS - 1, row_roll(south, -1), 0.0)
        put(pay, z.sec_sums + k, value)
        cols = jnp.where(lane == k, lane_roll(east, k - (LANES - 1)), cols)
        cols = jnp.where(lane == SUMS + k, lane_roll(west, SUMS + k), cols)
        pay[pl.ds(z.sec_rows * ROWS + k, 1), :] = north[ROWS - 1 :]
        pay[pl.ds(z.sec_rows * ROWS + SUMS + k, 1), :] = south[:1]
    put(pay, z.sec_cols, cols)
    spare = (z.sec_tiles - z.sec_rows) * ROWS - 2 * SUMS
    if spare:
        pay[pl.ds(z.sec_tiles * ROWS - spare, spare), :] = jnp.zeros((spare, LANES), F32)


def columns_kernel(z, mine, other, local, ecol, wcol, second_rows, fields, coup, flux, to_east, to_west, second_out):
    lane, row = lanes(), rows()
    sec = lax.axis_index("sec")
    total = 2 * z.levels
    for comp in range(2):
        for level in range(z.levels):
            own = level + sec * (z.levels - 1 - 2 * level)
            far = z.levels + level + sec * (z.levels - 1 - 2 * level)
            fields[comp * total + own] = take(mine, comp * z.levels + level)
            fields[comp * total + far] = take(other, comp * z.levels + level)
    sea, diffusion = take(local, 0), take(local, 1)
    top = sec * (total - 1)
    zonal, meridional = fields[top], fields[total + top]
    sums = [take(mine, z.sec_sums + k) + take(other, z.sec_sums + k) for k in range(SUMS)]
    coupling = coupled(sums, zonal, meridional, sea)
    cols = take(mine, z.sec_cols) + take(other, z.sec_cols)
    put(flux, 0, cols)
    for t in range(z.sec_tiles - z.sec_rows):
        put(flux, 1 + t, take(mine, z.sec_rows + t) + take(other, z.sec_rows + t))
    for k in range(4):
        coup[k] = coupling[k]
    arrays = [fields[k] for k in range(z.fields)] + [sea, diffusion] + coupling
    east, west = lane_roll(cols, z.lon_flux), lane_roll(cols, z.lon_flux - SUMS)
    for k, array in enumerate(arrays):
        mine_here = (lane >= HALO * k) & (lane < HALO * (k + 1))
        east = jnp.where(mine_here, lane_roll(array, HALO * (k + 1)), east)
        west = jnp.where(mine_here, lane_roll(array, HALO * k), west)
    for k in range(SUMS):
        edge = jnp.where(row == ROWS - 1, spread(flux, ROWS + k), spread(flux, ROWS + SUMS + k))
        at = z.lon_rows + FLUX_COLS * k
        mine_here = (lane >= at) & (lane < at + FLUX_COLS)
        east = jnp.where(mine_here, lane_roll(edge, at + FLUX_COLS), east)
        west = jnp.where(mine_here, lane_roll(edge, at), west)
    put(to_east, 0, east)
    put(to_west, 0, west)
    for t in range(z.col_tiles):
        put(to_east, 1 + t, take(ecol, t))
        put(to_west, 1 + t, take(wcol, t))
    second_out[...] = second_rows[...]


def rows_kernel(z, from_west, from_east, fields, coup, flux, local, coup_out, edges, to_first, to_second):
    lane, row = lanes(), rows()
    total = 2 * z.levels
    top = lax.axis_index("sec") * (total - 1)
    sea, diffusion = take(local, 0), take(local, 1)
    cols = take(flux, 0)
    west, east = take(from_west, 0), take(from_east, 0)

    def beyond(first, width):
        near = lane_roll(east, -first)
        far = lane_roll(west, LANES - width - first)
        return jnp.where(lane < width, near, jnp.where(lane >= LANES - width, far, 0.0))

    edge = [beyond(HALO * k, HALO) for k in range(z.fields + 2)]
    for k in range(z.fields + 2):
        edges[k] = edge[k]
    inner, outer = [], []
    for k in range(SUMS):
        at = z.lon_flux + k
        inner.append(jnp.where(lane == 0, lane_roll(west, -at), jnp.where(lane == LANES - 1, lane_roll(east, LANES - 1 - at), 0.0)))
        outer.append(jnp.where(lane == 0, lane_roll(cols, -k), jnp.where(lane == LANES - 1, lane_roll(cols, LANES - 1 - SUMS - k), 0.0)))
    inside = coupled(inner, fields[top], fields[total + top], sea)
    outside = coupled(outer, edges[top], edges[total + top], edge[z.fields])
    main_coupling = [coup[k] + inside[k] for k in range(4)]
    edge_coupling = [beyond(z.lon_coup + HALO * k, HALO) + outside[k] for k in range(4)]
    for k in range(4):
        coup_out[k] = main_coupling[k]
        edges[z.fields + 2 + k] = edge_coupling[k]
    row_edge = [beyond(z.lon_rows + FLUX_COLS * k, FLUX_COLS) for k in range(SUMS)]
    for k in range(SUMS):
        edges[z.arrays + k] = row_edge[k]

    main = [fields[k] for k in range(z.fields)] + [sea, diffusion] + main_coupling
    edge = edge + edge_coupling
    low = row < HALO
    odd = lax.rem(lax.axis_index("lat"), 2) == 1

    def send(index, north, south):
        put(to_first, index, jnp.where(odd, south, north))
        put(to_second, index, jnp.where(odd, north, south))

    def pair(a, b):
        return jnp.where(low, row_roll(b, HALO), a), jnp.where(low, a, row_roll(b, HALO))

    def group(tile, k):
        at = 2 * HALO * k
        in_group = lax.rem(lane + LANES + HALO - at, LANES) < 2 * HALO
        return in_group, lane_roll(tile, at)

    north_edges = jnp.zeros((ROWS, LANES), F32)
    south_edges = north_edges
    for k in range(z.pairs):
        north, south = pair(main[2 * k], main[2 * k + 1])
        send(z.lat_pairs + k, north, south)
        north, south = pair(edge[2 * k], edge[2 * k + 1])
        in_group, moved = group(north, k)
        north_edges = jnp.where(in_group, moved, north_edges)
        in_group, moved = group(south, k)
        south_edges = jnp.where(in_group, moved, south_edges)
    for t in range(z.flux_tiles):
        north, south = jnp.zeros((ROWS, LANES), F32), jnp.zeros((ROWS, LANES), F32)
        north_row, south_row = north, south
        for r in range(min(ROWS, SUMS - t * ROWS)):
            k = t * ROWS + r
            north = jnp.where(row == r, spread(flux, ROWS + k), north)
            south = jnp.where(row == r, spread(flux, ROWS + SUMS + k), south)
            north_row = jnp.where(row == r, jnp.broadcast_to(row_edge[k][ROWS - 1 :], (ROWS, LANES)), north_row)
            south_row = jnp.where(row == r, jnp.broadcast_to(row_edge[k][:1], (ROWS, LANES)), south_row)
        send(z.lat_flux + t, north, south)
        in_group, moved = group(north_row, z.pairs + t)
        north_edges = jnp.where(in_group, moved, north_edges)
        in_group, moved = group(south_row, z.pairs + t)
        south_edges = jnp.where(in_group, moved, south_edges)
    send(z.lat_edges, north_edges, south_edges)


def side_signs(j):
    return (1 if j in (0, 3) else -1), (1 if j in (0, 1) else -1)


def lat_sides(first, second, lat_count):
    place = lax.axis_index("lat")
    odd = lax.rem(place, 2) == 1
    north = jnp.where(place < lat_count - 1, jnp.where(odd, second, first), 0.0)
    south = jnp.where(place > 0, jnp.where(odd, first, second), 0.0)
    return north, south


def wave_kernel(z, lat_count, x, fields, coup, local, coef, from_west, from_east, first, second, out, coup_out, buf, scales, sides, sems):
    q, nf, half = z.quarter, z.freqs, z.half
    lane, row = lanes(), rows()
    total = 2 * z.levels
    top = lax.axis_index("sec") * (total - 1)
    sea = take(local, 0)
    zonal, meridional = current_gain * fields[top], current_gain * fields[total + top]
    coup_out[...] = coup[...]
    sides[0], sides[1] = lat_sides(first[...], second[...], lat_count)
    sizes = tables(z.directions)
    headings = []
    for i in range(q):
        c, s = float(sizes[0, i]), float(sizes[1, i])
        for j, heading in enumerate(z.headings(i)):
            sign_x, sign_y = side_signs(j)
            headings.append((heading, c, s, sign_x, sign_y, 2 * i + (0 if j in (0, 1) else 1)))
            scales[heading] = sea * (1.0 + (sign_x * c) * zonal + (sign_y * s) * meridional)

    def body(f, _):
        speed = spread(coef, f)
        at = pl.ds(pl.multiple_of((1 + lax.div(f, z.per_tile)) * ROWS, ROWS), ROWS)
        back = LANES - half * lax.rem(f, z.per_tile)
        west, east = lane_roll(from_west[at, :], back), lane_roll(from_east[at, :], back)
        for heading, c, s, sign_x, sign_y, k in headings:
            energy = x[f, heading]
            if sign_x > 0:
                beside = jnp.where(lane == 0, lane_roll(west, -k), lane_roll(energy, 1))
            else:
                beside = jnp.where(lane == LANES - 1, lane_roll(east, LANES - 1 - k), lane_roll(energy, -1))
            if sign_y > 0:
                below = jnp.where(row == 0, spread(sides.at[1], f * half + heading), row_roll(energy, 1))
            else:
                below = jnp.where(row == ROWS - 1, spread(sides.at[0], f * half + heading - half), row_roll(energy, -1))
            step = c * (beside - energy) + s * (below - energy)
            buf[f, heading] = scales[heading] * (energy + speed * step)
        return 0

    parts = 3 if nf % 3 == 0 else 1
    copies = []
    for g in range(parts):
        span = pl.ds(g * (nf // parts), nf // parts)
        lax.fori_loop(g * (nf // parts), (g + 1) * (nf // parts), body, 0)
        copy = pltpu.make_async_copy(buf.at[span], out.at[span], sems.at[g])
        copy.start()
        copies.append(copy)
    for copy in copies:
        copy.wait()


def ocean_kernel(z, lat_count, from_first, from_second, fields, coup, flux, edges, local, currents_out, ext, force):
    total = 2 * z.levels
    row = rows()
    sec = lax.axis_index("sec")
    top = sec * (total - 1)
    sea, diffusion = take(local, 0), take(local, 1)
    low = row < HALO

    def pair(north, south):
        first = jnp.where(low, north, south)
        second = jnp.where(low, row_roll(north, HALO), row_roll(south, HALO))
        return first, second

    def sides(index):
        return lat_sides(take(from_first, index), take(from_second, index), lat_count)

    north_edges, south_edges = sides(z.lat_edges)
    north_rows, south_rows = zip(*[sides(z.lat_flux + t) for t in range(z.flux_tiles)])
    halo, halo_edge = [], []
    for k in range(z.pairs):
        halo += pair(*sides(z.lat_pairs + k))
        halo_edge += pair(lane_roll(north_edges, -2 * HALO * k), lane_roll(south_edges, -2 * HALO * k))
    inner, outer, inner_edge, outer_edge = [], [], [], []
    for k in range(SUMS):
        t, r = k // ROWS, k % ROWS
        high = row == ROWS - 1
        bottom = row == 0
        north = jnp.broadcast_to(north_rows[t][r : r + 1], (ROWS, LANES))
        south = jnp.broadcast_to(south_rows[t][r : r + 1], (ROWS, LANES))
        inner.append(jnp.where(high, north, jnp.where(bottom, south, 0.0)))
        outer.append(jnp.where(bottom, spread(flux, ROWS + k), jnp.where(high, spread(flux, ROWS + SUMS + k), 0.0)))
        shift = -2 * HALO * (z.pairs + t)
        north = jnp.broadcast_to(lane_roll(north_edges, shift)[r : r + 1], (ROWS, LANES))
        south = jnp.broadcast_to(lane_roll(south_edges, shift)[r : r + 1], (ROWS, LANES))
        inner_edge.append(jnp.where(high, north, jnp.where(bottom, south, 0.0)))
        mine = edges[z.arrays + k]
        outer_edge.append(
            jnp.where(bottom, jnp.broadcast_to(mine[ROWS - 1 :], (ROWS, LANES)), jnp.where(high, jnp.broadcast_to(mine[:1], (ROWS, LANES)), 0.0))
        )

    def joined(main, edge, halo_main, halo_side):
        return jnp.concatenate([jnp.concatenate([main, edge], axis=1), jnp.concatenate([halo_main, halo_side], axis=1)], axis=0)

    for k in range(z.fields):
        ext[k] = joined(fields[k], edges[k], halo[k], halo_edge[k])
    sea_all = joined(sea, edges[z.fields], halo[z.fields], halo_edge[z.fields])
    kappa = joined(diffusion, edges[z.fields + 1], halo[z.fields + 1], halo_edge[z.fields + 1])
    sums = [joined(inner[k], inner_edge[k], outer[k], outer_edge[k]) for k in range(SUMS)]
    extra = coupled(sums, ext[top], ext[total + top], sea_all)
    first = z.fields + 2
    coupling = [joined(coup[k], edges[first + k], halo[first + k], halo_edge[first + k]) + extra[k] for k in range(4)]

    shape = (2 * ROWS, 2 * LANES)
    row_all = lax.broadcasted_iota(jnp.int32, shape, 0)
    row_all = jnp.where(row_all >= 2 * ROWS - HALO, row_all - 2 * ROWS, row_all) + lax.axis_index("lat") * ROWS
    rot = sea_all * (0.05 + 0.1 * (row_all.astype(F32) + 0.5) / (lat_count * ROWS))
    spin = sea_all * kappa

    def level_of(p):
        return p + sec * (total - 1 - 2 * p)

    mixes, centers = [], []
    for p in range(total):
        level = level_of(p)
        mixes.append(0.04 + 0.0125 * lax.rem(7 * level, 5).astype(F32))
        decay = 1.0 / (1.0 + jnp.full(shape, level, jnp.int32).astype(F32))
        gain = jnp.where(level == 0, stress_gain, 0.0)
        force[p] = rot * decay * coupling[1] + sea_all * gain * coupling[2]
        force[total + p] = sea_all * gain * coupling[3] - rot * decay * coupling[0]
    for step in range(ITERS):
        needed = min(total, z.levels + ITERS - 1 - step)
        after = []
        for comp in range(2):
            for p in range(needed):
                value = ext[comp * total + p]
                ring = (pltpu.roll(value, 1, 1) + pltpu.roll(value, 2 * LANES - 1, 1)) + (pltpu.roll(value, 1, 0) + pltpu.roll(value, 2 * ROWS - 1, 0))
                near = [ext[comp * total + other] for other in (p - 1, p + 1) if 0 <= other < total]
                column = near[0] - value if len(near) == 1 else near[0] + near[1] - 2.0 * value
                turned = ext[(1 - comp) * total + p]
                turned = rot * turned if comp == 0 else -(rot * turned)
                after.append(sea_all * (value + mixes[p] * column) + spin * (ring - 4.0 * value) + turned + force[comp * total + p])
        if step < ITERS - 1:
            for comp in range(2):
                for p in range(needed):
                    ext[comp * total + p] = after[comp * needed + p]
        else:
            for comp in range(2):
                for level in range(z.levels):
                    own = level
                    place = level + sec * (z.levels - 1 - 2 * level)
                    currents_out[comp, place] = after[comp * needed + own][:ROWS, :LANES]


def tables(directions):
    quarter = directions // 4
    heading = (np.arange(quarter) + 0.5) * (2.0 * math.pi / directions)
    return np.stack([np.cos(heading), np.sin(heading)]).astype(np.float32)


def shifted(value, axis, steps):
    count = lax.axis_size(axis)
    return lax.ppermute(value, axis, [(i, (i + steps) % count) for i in range(count)])


def swapped(value, parity):
    lat, lon = lax.axis_size("lat"), lax.axis_size("lon")
    pairs = []
    for i in range(lat):
        other = i + 1 if i % 2 == parity else i - 1
        for j in range(lon):
            if 0 <= other < lat:
                pairs.append((i * lon + j, other * lon + j))
            elif j ^ 1 < lon:
                pairs.append((i * lon + j, i * lon + (j ^ 1)))
    return lax.ppermute(value, ("lat", "lon"), pairs)


def flat(tiles):
    return jax.ShapeDtypeStruct((tiles * ROWS, LANES), F32)


def stack(count):
    return jax.ShapeDtypeStruct((count, ROWS, LANES), F32)


def call(kernel, out_shape, in_specs, out_specs=None, scratch=(), name=None, bytes_accessed=0, flops=0):
    return pl.pallas_call(
        kernel,
        out_shape=out_shape,
        in_specs=in_specs,
        out_specs=out_specs if out_specs is not None else [VMEM] * len(out_shape),
        scratch_shapes=list(scratch),
        name=name,
        compiler_params=pltpu.CompilerParams(vmem_limit_bytes=24 * 1024 * 1024),
        cost_estimate=pl.CostEstimate(flops=flops, bytes_accessed=bytes_accessed, transcendentals=0),
    )


def shards(spectra, currents, land_mask, diffusion, courant, stokes_weight, stress_weight):
    freqs, directions, tile_rows, tile_cols = spectra.shape
    levels = currents.shape[1]
    lat_count = lax.axis_size("lat")
    assert lax.axis_size("sec") == 2 and (tile_rows, tile_cols) == (ROWS, LANES) and directions % 4 == 0
    z = Sizes(freqs, directions, levels)
    table = jnp.asarray(tables(directions))
    size = spectra.size * 4
    copies = 4 * len(chunks(z))
    sems = pltpu.SemaphoreType.DMA((copies,))
    whole = pltpu.VMEM(spectra.shape, F32)

    edge_rows = jax.ShapeDtypeStruct((z.edge_rows, LANES), F32)
    inputs = (spectra, currents, land_mask, diffusion, courant, stokes_weight, stress_weight, table)
    kept, pay, first_rows, second_rows, ecol, wcol, local, coef = call(
        functools.partial(sums_kernel, z),
        (whole, flat(z.sec_tiles), edge_rows, edge_rows, flat(z.col_tiles), flat(z.col_tiles), flat(2), flat(z.coef_tiles)),
        [ANY] * 8,
        scratch=[
            pltpu.VMEM(currents.shape, F32),
            pltpu.VMEM(land_mask.shape, jnp.int32),
            pltpu.SMEM(courant.shape, F32),
            pltpu.SMEM(courant.shape, F32),
            pltpu.SMEM(courant.shape, F32),
            pltpu.SMEM(table.shape, F32),
            pltpu.VMEM((5 * SUMS, ROWS, LANES), F32),
            sems,
            pltpu.SemaphoreType.DMA((7,)),
        ],
        name="spectra_sums",
        bytes_accessed=size,
        flops=16 * size // 4,
    )(*[pltpu.with_memory_space_constraint(array, pltpu.HBM) for array in inputs])

    got_first = swapped(first_rows, 0)
    other = shifted(pay, "sec", 1)

    fields, coup, flux, to_east, to_west, second_rows = call(
        functools.partial(columns_kernel, z),
        (stack(z.fields), stack(4), flat(1 + z.sec_tiles - z.sec_rows), flat(1 + z.col_tiles), flat(1 + z.col_tiles), edge_rows),
        [VMEM] * 6,
        name="pack_columns",
        bytes_accessed=2**18,
        flops=2**16,
    )(pay, other, local, ecol, wcol, second_rows)

    got_second = swapped(second_rows, 1)
    from_east = shifted(to_west, "lon", -1)
    from_west = shifted(to_east, "lon", 1)

    coup, edges, to_first, to_second = call(
        functools.partial(rows_kernel, z),
        (stack(4), stack(z.arrays + SUMS), flat(z.lat_tiles), flat(z.lat_tiles)),
        [VMEM] * 6,
        name="pack_rows",
        bytes_accessed=2**18,
        flops=2**16,
    )(from_west, from_east, fields, coup, flux, local)

    from_second = swapped(to_second, 1)
    from_first = swapped(to_first, 0)

    new_spectra, coup = call(
        functools.partial(wave_kernel, z, lat_count),
        (jax.ShapeDtypeStruct(spectra.shape, F32), stack(4)),
        [VMEM] * 9,
        out_specs=[ANY, VMEM],
        scratch=[whole, pltpu.VMEM((directions, ROWS, LANES), F32), pltpu.VMEM((2, z.edge_rows, LANES), F32), sems],
        name="wave_step",
        bytes_accessed=2 * size,
        flops=9 * size // 4,
    )(kept, fields, coup, local, coef, from_west, from_east, got_first, got_second)

    (new_currents,) = call(
        functools.partial(ocean_kernel, z, lat_count),
        (jax.ShapeDtypeStruct(currents.shape, F32),),
        [VMEM] * 7,
        scratch=[pltpu.VMEM((z.fields, 2 * ROWS, 2 * LANES), F32), pltpu.VMEM((z.fields, 2 * ROWS, 2 * LANES), F32)],
        name="ocean_steps",
        bytes_accessed=2**20,
        flops=2**20,
    )(from_first, from_second, fields, coup, flux, edges, local)
    return new_spectra, new_currents


def solution(mesh):
    in_specs = (
        P("sec", None, "lat", "lon"),
        P(None, "sec", "lat", "lon"),
        P("lat", "lon"),
        P("lat", "lon"),
        P("sec"),
        P("sec"),
        P("sec"),
    )
    out_specs = (P("sec", None, "lat", "lon"), P(None, "sec", "lat", "lon"))
    return jax.shard_map(shards, mesh=mesh, in_specs=in_specs, out_specs=out_specs, check_vma=False)
```

```python
import functools
import math

import jax
import jax.numpy as jnp
import numpy as np
from jax import lax
from jax.experimental import pallas as pl
from jax.experimental.pallas import tpu as pltpu
from jax.sharding import PartitionSpec as P

ITERS = 4
ROWS = 8
LANES = 128
HALO = 4
MOMENTS = 5
SUMS = 2 * MOMENTS
FLUX_COLS = 3
current_gain = 0.1
stress_gain = 0.5

VMEM = pl.BlockSpec(memory_space=pltpu.VMEM)
SMEM = pl.BlockSpec(memory_space=pltpu.SMEM)
ANY = pl.BlockSpec(memory_space=pl.ANY)
F32 = jnp.float32
BF16 = jnp.bfloat16


def lanes():
    return lax.broadcasted_iota(jnp.int32, (ROWS, LANES), 1)


def rows():
    return lax.broadcasted_iota(jnp.int32, (ROWS, LANES), 0)


def lane_roll(tile, shift):
    if isinstance(shift, int):
        shift %= LANES
        if shift == 0:
            return tile
    return pltpu.roll(tile, shift, 1)


def row_roll(tile, shift):
    shift %= ROWS
    return tile if shift == 0 else pltpu.roll(tile, shift, 0)


def spread(ref, row):
    return jnp.broadcast_to(ref[pl.ds(row, 1), :], (ROWS, LANES))


def put(ref, index, tile):
    ref[pl.ds(index * ROWS, ROWS), :] = tile


def take(ref, index):
    return ref[pl.ds(index * ROWS, ROWS), :]


def coupled(sums, zonal, meridional, sea):
    result = []
    for w in range(2):
        c, s, cc, cs, ss = sums[w * MOMENTS : (w + 1) * MOMENTS]
        result.append(sea * (c + current_gain * (zonal * cc + meridional * cs)))
        result.append(sea * (s + current_gain * (zonal * cs + meridional * ss)))
    return result


class Sizes:
    def __init__(self, freqs, directions, levels):
        self.freqs = freqs
        self.directions = directions
        self.levels = levels
        self.quarter = directions // 4
        self.fields = 2 * 2 * levels
        self.half = directions // 2
        self.per_tile = LANES // self.half
        self.col_tiles = -(-freqs // self.per_tile)
        self.edge_rows = freqs * directions // 2
        self.sec_sums = self.fields // 2
        self.sec_cols = self.sec_sums + SUMS
        self.sec_rows = self.sec_cols + 1
        self.sec_tiles = self.sec_rows + -(-2 * SUMS // ROWS)
        self.lon_coup = HALO * (self.fields + 2)
        self.lon_flux = self.lon_coup + 4 * HALO
        self.lon_rows = self.lon_flux + SUMS
        self.arrays = self.fields + 2 + 4
        self.pairs = self.arrays // 2
        self.flux_tiles = -(-SUMS // ROWS)
        self.lat_pairs = 0
        self.lat_flux = self.lat_pairs + self.pairs
        self.lat_edges = self.lat_flux + self.flux_tiles
        self.lat_tiles = self.lat_edges + 1
        self.coef_tiles = -(-freqs // ROWS)
        assert self.lon_rows + SUMS * FLUX_COLS <= LANES
        assert (self.pairs + self.flux_tiles) * 2 * HALO <= LANES

    def headings(self, i):
        q = self.quarter
        return (i, 2 * q - 1 - i, 2 * q + i, 4 * q - 1 - i)


def chunks(z):
    q = z.quarter
    group = 3 if q % 3 == 0 else 1
    result = []
    for lo in range(0, q, group):
        hi = lo + group
        result.append((lo, hi, [pl.ds(start, group) for start in (lo, 2 * q - hi, 2 * q + lo, 4 * q - hi)]))
    return result


def sums_kernel(z, x, cur_in, mask_in, diffusion_in, courant_in, stokes_in, stress_in, buf, pay, ecol, wcol, local, coef, cur, mask, courant, stokes, stress, acc, sems, small_sems):
    q, nf = z.quarter, z.freqs
    pairs = ((cur_in, cur), (mask_in, mask), (diffusion_in, local.at[pl.ds(ROWS, ROWS)]), (courant_in, courant), (stokes_in, stokes), (stress_in, stress))
    small = [pltpu.make_async_copy(source, target, small_sems.at[k]) for k, (source, target) in enumerate(pairs)]
    for copy in small:
        copy.start()
    copies = []
    for g, (_, _, spans) in enumerate(chunks(z)):
        for j, span in enumerate(spans):
            copies.append(pltpu.make_async_copy(x.at[:, span], buf.at[:, span], sems.at[4 * g + j]))
    for copy in copies:
        copy.start()

    lane, row = lanes(), rows()
    zero = jnp.zeros((ROWS, LANES), F32)
    for k in range(5 * SUMS):
        acc[k] = zero
    sizes = tables(z.directions)
    east, west = [zero] * z.col_tiles, [zero] * z.col_tiles
    for copy in small:
        copy.wait()
    sea = mask[...].astype(F32)
    put(local, 0, sea)
    for comp in range(2):
        for level in range(z.levels):
            put(pay, comp * z.levels + level, cur[comp, level] * sea)
    for f in range(nf):
        coef[pl.ds(f, 1), :] = jnp.full((1, LANES), courant[f], F32)

    def add(i):
        c, s = float(sizes[0, i]), float(sizes[1, i])
        heading = z.headings(i)
        total = [[zero] * 4 for _ in range(4)]
        for f in range(nf):
            t = f // z.per_tile
            cg = courant[f]
            factors = (stokes[f], stokes[f] * cg, stress[f], stress[f] * cg)
            for j in range(4):
                energy = buf[f, heading[j]]
                for k in range(4):
                    total[k][j] = total[k][j] + factors[k] * energy
                at = f % z.per_tile * z.half + 2 * i + (0 if j in (0, 1) else 1)
                if j in (0, 3):
                    east[t] = jnp.where(lane == at, lane_roll(energy, at - (LANES - 1)), east[t])
                else:
                    west[t] = jnp.where(lane == at, lane_roll(energy, at), west[t])
        cc, cs, ss = c * c, c * s, s * s
        for w in range(2):
            plain, fast = total[2 * w], total[2 * w + 1]
            both = c + s
            h = [plain[j] - both * fast[j] for j in range(4)]
            here, there = h[0] + h[3], h[1] + h[2]
            every = here + there
            values = [
                c * (here - there),
                s * ((h[0] + h[1]) - (h[2] + h[3])),
                cc * every,
                cs * ((h[0] - h[3]) + (h[2] - h[1])),
                ss * every,
            ]
            for a, b, size, signs in (
                (fast[0] + fast[3], fast[0] - fast[3], c, (1, 1, 1)),
                (fast[1] + fast[2], fast[1] - fast[2], c, (-1, 1, -1)),
            ):
                values += [signs[0] * size * c * a, signs[1] * size * s * b, size * cc * a, signs[2] * size * cs * b, size * ss * a]
            for a, b, size, signs in (
                (fast[0] + fast[1], fast[0] - fast[1], s, (1, 1, 1)),
                (fast[2] + fast[3], fast[3] - fast[2], s, (1, -1, -1)),
            ):
                values += [signs[0] * size * c * b, signs[1] * size * s * a, size * cc * a, signs[2] * size * cs * b, size * ss * a]
            for kind in range(5):
                for m in range(MOMENTS):
                    at = kind * SUMS + w * MOMENTS + m
                    acc[at] = acc[at] + values[kind * MOMENTS + m]

    for g, (lo, hi, _) in enumerate(chunks(z)):
        for copy in copies[4 * g : 4 * g + 4]:
            copy.wait()
        for i in range(lo, hi):
            add(i)
    for t in range(z.col_tiles):
        put(ecol, t, east[t])
        put(wcol, t, west[t])

    cols = zero
    for k in range(SUMS):
        center, east, west, north, south = (acc[kind * SUMS + k] for kind in range(5))
        value = center + jnp.where(lane > 0, lane_roll(east, 1), 0.0) + jnp.where(lane < LANES - 1, lane_roll(west, -1), 0.0)
        value = value + jnp.where(row > 0, row_roll(north, 1), 0.0) + jnp.where(row < ROWS - 1, row_roll(south, -1), 0.0)
        put(pay, z.sec_sums + k, value)
        cols = jnp.where(lane == k, lane_roll(east, k - (LANES - 1)), cols)
        cols = jnp.where(lane == SUMS + k, lane_roll(west, SUMS + k), cols)
        pay[pl.ds(z.sec_rows * ROWS + k, 1), :] = north[ROWS - 1 :]
        pay[pl.ds(z.sec_rows * ROWS + SUMS + k, 1), :] = south[:1]
    put(pay, z.sec_cols, cols)
    spare = (z.sec_tiles - z.sec_rows) * ROWS - 2 * SUMS
    if spare:
        pay[pl.ds(z.sec_tiles * ROWS - spare, spare), :] = jnp.zeros((spare, LANES), F32)


def parts(tile):
    high = tile.astype(BF16).astype(F32)
    return high, (tile - high).astype(BF16).astype(F32)


def edge_rows_kernel(z, x, first_rows, second_rows):
    flat = x.reshape(z.freqs * z.directions * ROWS, LANES)
    odd = lax.rem(lax.axis_index("lat"), 2)
    north, south = ROWS - 1, z.half * ROWS
    for ref, start in ((first_rows, north + odd * (south - north)), (second_rows, south + odd * (north - south))):
        for f in range(z.freqs):
            ref[pl.ds(f * z.half, z.half), :] = flat[pl.ds(f * z.directions * ROWS + start, z.half, stride=ROWS), :]


def matrices_kernel(z, x, picks, beside):
    lane = lanes()
    for k in range(z.half // 2):
        both = [((lane & (LANES // 2 - 1)) == 2 * k + n).astype(F32) for n in range(2)]
        picks[pl.ds(2 * ROWS * k, 2 * ROWS), :] = jnp.concatenate(both, axis=0).astype(BF16)
    shape = (2 * LANES, 2 * LANES)
    apart = lax.broadcasted_iota(jnp.int32, shape, 0) - lax.broadcasted_iota(jnp.int32, shape, 1)
    apart = apart & (2 * LANES - 1)
    beside[...] = ((apart == 1) | (apart == 2 * LANES - 1)).astype(F32).astype(BF16)


def columns_kernel(z, mine, other, picks, local, ecol, wcol, fields, coup, flux, to_east, to_west):
    lane, row = lanes(), rows()
    sec = lax.axis_index("sec")
    total = 2 * z.levels
    for comp in range(2):
        for level in range(z.levels):
            own = level + sec * (z.levels - 1 - 2 * level)
            far = z.levels + level + sec * (z.levels - 1 - 2 * level)
            fields[comp * total + own] = take(mine, comp * z.levels + level)
            fields[comp * total + far] = take(other, comp * z.levels + level)
    sea, diffusion = take(local, 0), take(local, 1)
    top = sec * (total - 1)
    zonal, meridional = fields[top], fields[total + top]
    sums = [take(mine, z.sec_sums + k) + take(other, z.sec_sums + k) for k in range(SUMS)]
    coupling = coupled(sums, zonal, meridional, sea)
    cols = take(mine, z.sec_cols) + take(other, z.sec_cols)
    put(flux, 0, cols)
    for t in range(z.sec_tiles - z.sec_rows):
        put(flux, 1 + t, take(mine, z.sec_rows + t) + take(other, z.sec_rows + t))
    for k in range(4):
        coup[k] = coupling[k]
    arrays = [fields[k] for k in range(z.fields)] + [sea, diffusion] + coupling
    east, west = lane_roll(cols, z.lon_flux), lane_roll(cols, z.lon_flux - SUMS)
    for k, array in enumerate(arrays):
        mine_here = (lane >= HALO * k) & (lane < HALO * (k + 1))
        east = jnp.where(mine_here, lane_roll(array, HALO * (k + 1)), east)
        west = jnp.where(mine_here, lane_roll(array, HALO * k), west)
    for k in range(SUMS):
        edge = jnp.where(row == ROWS - 1, spread(flux, ROWS + k), spread(flux, ROWS + SUMS + k))
        at = z.lon_rows + FLUX_COLS * k
        mine_here = (lane >= at) & (lane < at + FLUX_COLS)
        east = jnp.where(mine_here, lane_roll(edge, at + FLUX_COLS), east)
        west = jnp.where(mine_here, lane_roll(edge, at), west)
    put(to_east, 0, east)
    put(to_west, 0, west)
    for t in range(z.col_tiles):
        put(to_east, 1 + t, take(ecol, t))
        put(to_west, 1 + t, take(wcol, t))


def rows_kernel(z, from_west, from_east, fields, coup, flux, local, coup_out, edges, to_first, to_second):
    lane, row = lanes(), rows()
    total = 2 * z.levels
    top = lax.axis_index("sec") * (total - 1)
    sea, diffusion = take(local, 0), take(local, 1)
    cols = take(flux, 0)
    west, east = take(from_west, 0), take(from_east, 0)

    def beyond(first, width):
        near = lane_roll(east, -first)
        far = lane_roll(west, LANES - width - first)
        return jnp.where(lane < width, near, jnp.where(lane >= LANES - width, far, 0.0))

    edge = [beyond(HALO * k, HALO) for k in range(z.fields + 2)]
    for k in range(z.fields + 2):
        edges[k] = edge[k]
    inner, outer = [], []
    for k in range(SUMS):
        at = z.lon_flux + k
        inner.append(jnp.where(lane == 0, lane_roll(west, -at), jnp.where(lane == LANES - 1, lane_roll(east, LANES - 1 - at), 0.0)))
        outer.append(jnp.where(lane == 0, lane_roll(cols, -k), jnp.where(lane == LANES - 1, lane_roll(cols, LANES - 1 - SUMS - k), 0.0)))
    inside = coupled(inner, fields[top], fields[total + top], sea)
    outside = coupled(outer, edges[top], edges[total + top], edge[z.fields])
    main_coupling = [coup[k] + inside[k] for k in range(4)]
    edge_coupling = [beyond(z.lon_coup + HALO * k, HALO) + outside[k] for k in range(4)]
    for k in range(4):
        coup_out[k] = main_coupling[k]
        edges[z.fields + 2 + k] = edge_coupling[k]
    row_edge = [beyond(z.lon_rows + FLUX_COLS * k, FLUX_COLS) for k in range(SUMS)]
    for k in range(SUMS):
        edges[z.arrays + k] = row_edge[k]

    main = [fields[k] for k in range(z.fields)] + [sea, diffusion] + main_coupling
    edge = edge + edge_coupling
    low = row < HALO
    odd = lax.rem(lax.axis_index("lat"), 2) == 1

    def send(index, north, south):
        put(to_first, index, jnp.where(odd, south, north))
        put(to_second, index, jnp.where(odd, north, south))

    def pair(a, b):
        return jnp.where(low, row_roll(b, HALO), a), jnp.where(low, a, row_roll(b, HALO))

    def group(tile, k):
        at = 2 * HALO * k
        in_group = lax.rem(lane + LANES + HALO - at, LANES) < 2 * HALO
        return in_group, lane_roll(tile, at)

    north_edges = jnp.zeros((ROWS, LANES), F32)
    south_edges = north_edges
    for k in range(z.pairs):
        north, south = pair(main[2 * k], main[2 * k + 1])
        send(z.lat_pairs + k, north, south)
        north, south = pair(edge[2 * k], edge[2 * k + 1])
        in_group, moved = group(north, k)
        north_edges = jnp.where(in_group, moved, north_edges)
        in_group, moved = group(south, k)
        south_edges = jnp.where(in_group, moved, south_edges)
    for t in range(z.flux_tiles):
        north, south = jnp.zeros((ROWS, LANES), F32), jnp.zeros((ROWS, LANES), F32)
        north_row, south_row = north, south
        for r in range(min(ROWS, SUMS - t * ROWS)):
            k = t * ROWS + r
            north = jnp.where(row == r, spread(flux, ROWS + k), north)
            south = jnp.where(row == r, spread(flux, ROWS + SUMS + k), south)
            north_row = jnp.where(row == r, jnp.broadcast_to(row_edge[k][ROWS - 1 :], (ROWS, LANES)), north_row)
            south_row = jnp.where(row == r, jnp.broadcast_to(row_edge[k][:1], (ROWS, LANES)), south_row)
        send(z.lat_flux + t, north, south)
        in_group, moved = group(north_row, z.pairs + t)
        north_edges = jnp.where(in_group, moved, north_edges)
        in_group, moved = group(south_row, z.pairs + t)
        south_edges = jnp.where(in_group, moved, south_edges)
    send(z.lat_edges, north_edges, south_edges)


def side_signs(j):
    return (1 if j in (0, 3) else -1), (1 if j in (0, 1) else -1)


def lat_sides(first, second, lat_count):
    place = lax.axis_index("lat")
    odd = lax.rem(place, 2) == 1
    north = jnp.where(place < lat_count - 1, jnp.where(odd, second, first), 0.0)
    south = jnp.where(place > 0, jnp.where(odd, first, second), 0.0)
    return north, south


def wave_kernel(z, lat_count, x, fields, coup, local, coef, picks, from_west, from_east, first, second, out, coup_out, buf, scales, sides, sems):
    q, nf, half = z.quarter, z.freqs, z.half
    lane, row = lanes(), rows()
    total = 2 * z.levels
    top = lax.axis_index("sec") * (total - 1)
    sea = take(local, 0)
    zonal, meridional = current_gain * fields[top], current_gain * fields[total + top]
    coup_out[...] = coup[...]
    sides[0], sides[1] = lat_sides(first[...], second[...], lat_count)
    sizes = tables(z.directions)
    headings = []
    for i in range(q):
        c, s = float(sizes[0, i]), float(sizes[1, i])
        for j, heading in enumerate(z.headings(i)):
            sign_x, sign_y = side_signs(j)
            headings.append((heading, i, sign_x, sign_y, 2 * i + (0 if j in (0, 1) else 1)))
            scales[heading] = sea * (1.0 + (sign_x * c) * zonal + (sign_y * s) * meridional)
    ones = jnp.ones((LANES, LANES), BF16)

    def body(f, _):
        speed = spread(coef, f)
        along = [speed * float(sizes[0, i]) for i in range(q)]
        across = [speed * float(sizes[1, i]) for i in range(q)]
        stay = [1.0 - along[i] - across[i] for i in range(q)]
        at = pl.ds(pl.multiple_of((1 + (f // z.per_tile)) * ROWS, ROWS), ROWS)
        back = LANES - half * (f % z.per_tile)
        rims = []
        for ref in (from_west, from_east):
            high, low = parts(lane_roll(ref[at, :], back))
            both = jnp.where(lane < LANES // 2, high, lane_roll(low, LANES // 2))
            both = jnp.concatenate([both, both], axis=0).astype(BF16)
            chosen = jnp.concatenate([both] * (half // 2), axis=0) * picks[...]
            rims.append(jnp.dot(chosen, ones, preferred_element_type=F32))
        for heading, i, sign_x, sign_y, k in headings:
            energy = x[f, heading]
            if sign_x > 0:
                beside = jnp.where(lane == 0, rims[0][k * ROWS : (k + 1) * ROWS], lane_roll(energy, 1))
            else:
                beside = jnp.where(lane == LANES - 1, rims[1][k * ROWS : (k + 1) * ROWS], lane_roll(energy, -1))
            if sign_y > 0:
                below = jnp.where(row == 0, spread(sides.at[1], f * half + heading), row_roll(energy, 1))
            else:
                below = jnp.where(row == ROWS - 1, spread(sides.at[0], f * half + heading - half), row_roll(energy, -1))
            buf[f, heading] = scales[heading] * (stay[i] * energy + along[i] * beside + across[i] * below)
        return 0

    count = 3 if nf % 3 == 0 else 1
    copies = []
    for g in range(count):
        span = pl.ds(g * (nf // count), nf // count)
        lax.fori_loop(g * (nf // count), (g + 1) * (nf // count), body, 0, unroll=6 if nf % 18 == 0 else 1)
        copy = pltpu.make_async_copy(buf.at[span], out.at[span], sems.at[g])
        copy.start()
        copies.append(copy)
    for copy in copies:
        copy.wait()


def ocean_kernel(z, lat_count, from_first, from_second, fields, coup, flux, edges, local, beside, currents_out, ext, force, still, mixed):
    total = 2 * z.levels
    row = rows()
    sec = lax.axis_index("sec")
    top = sec * (total - 1)
    sea, diffusion = take(local, 0), take(local, 1)
    low = row < HALO

    def pair(north, south):
        first = jnp.where(low, north, south)
        second = jnp.where(low, row_roll(north, HALO), row_roll(south, HALO))
        return first, second

    def sides(index):
        return lat_sides(take(from_first, index), take(from_second, index), lat_count)

    north_edges, south_edges = sides(z.lat_edges)
    north_rows, south_rows = zip(*[sides(z.lat_flux + t) for t in range(z.flux_tiles)])
    halo, halo_edge = [], []
    for k in range(z.pairs):
        halo += pair(*sides(z.lat_pairs + k))
        halo_edge += pair(lane_roll(north_edges, -2 * HALO * k), lane_roll(south_edges, -2 * HALO * k))
    inner, outer, inner_edge, outer_edge = [], [], [], []
    for k in range(SUMS):
        t, r = k // ROWS, k % ROWS
        high = row == ROWS - 1
        bottom = row == 0
        north = jnp.broadcast_to(north_rows[t][r : r + 1], (ROWS, LANES))
        south = jnp.broadcast_to(south_rows[t][r : r + 1], (ROWS, LANES))
        inner.append(jnp.where(high, north, jnp.where(bottom, south, 0.0)))
        outer.append(jnp.where(bottom, spread(flux, ROWS + k), jnp.where(high, spread(flux, ROWS + SUMS + k), 0.0)))
        shift = -2 * HALO * (z.pairs + t)
        north = jnp.broadcast_to(lane_roll(north_edges, shift)[r : r + 1], (ROWS, LANES))
        south = jnp.broadcast_to(lane_roll(south_edges, shift)[r : r + 1], (ROWS, LANES))
        inner_edge.append(jnp.where(high, north, jnp.where(bottom, south, 0.0)))
        mine = edges[z.arrays + k]
        outer_edge.append(
            jnp.where(bottom, jnp.broadcast_to(mine[ROWS - 1 :], (ROWS, LANES)), jnp.where(high, jnp.broadcast_to(mine[:1], (ROWS, LANES)), 0.0))
        )

    def joined(main, edge, halo_main, halo_side):
        return jnp.concatenate([jnp.concatenate([main, edge], axis=1), jnp.concatenate([halo_main, halo_side], axis=1)], axis=0)

    for k in range(z.fields):
        ext[k] = joined(fields[k], edges[k], halo[k], halo_edge[k])
    sea_all = joined(sea, edges[z.fields], halo[z.fields], halo_edge[z.fields])
    kappa = joined(diffusion, edges[z.fields + 1], halo[z.fields + 1], halo_edge[z.fields + 1])
    sums = [joined(inner[k], inner_edge[k], outer[k], outer_edge[k]) for k in range(SUMS)]
    extra = coupled(sums, ext[top], ext[total + top], sea_all)
    first = z.fields + 2
    coupling = [joined(coup[k], edges[first + k], halo[first + k], halo_edge[first + k]) + extra[k] for k in range(4)]

    shape = (2 * ROWS, 2 * LANES)
    row_all = lax.broadcasted_iota(jnp.int32, shape, 0)
    row_all = jnp.where(row_all >= 2 * ROWS - HALO, row_all - 2 * ROWS, row_all) + lax.axis_index("lat") * ROWS
    rot = sea_all * (0.05 + 0.1 * (row_all.astype(F32) + 0.5) * (1.0 / (lat_count * ROWS)))
    spin = sea_all * kappa

    def by_level(function, p):
        return jnp.where(sec == 0, function(p), function(total - 1 - p)).astype(F32)

    for p in range(total):
        mix, decay, gain = by_level(lambda level: 0.04 + 0.0125 * (7 * level % 5), p), by_level(lambda level: 1.0 / (1.0 + level), p), by_level(lambda level: stress_gain if level == 0 else 0.0, p)
        force[p] = rot * decay * coupling[1] + sea_all * gain * coupling[2]
        force[total + p] = sea_all * gain * coupling[3] - rot * decay * coupling[0]
        mixed[p] = sea_all * mix
        still[p] = sea_all * (1.0 - mix * (1 if p in (0, total - 1) else 2)) - 4.0 * spin
    for step in range(ITERS):
        needed = min(total, z.levels + ITERS - 1 - step)
        every = [ext[comp * total + p] for comp in range(2) for p in range(needed)]
        high, low = parts(jnp.concatenate(every, axis=0))
        ring = jnp.dot(high.astype(BF16), beside[...], preferred_element_type=F32)
        ring = ring + jnp.dot(low.astype(BF16), beside[...], preferred_element_type=F32)
        after = []
        for comp in range(2):
            for p in range(needed):
                at = comp * needed + p
                value = every[at]
                around = ring[2 * ROWS * at : 2 * ROWS * (at + 1)] + (pltpu.roll(value, 1, 0) + pltpu.roll(value, 2 * ROWS - 1, 0))
                near = [ext[comp * total + other] for other in (p - 1, p + 1) if 0 <= other < total]
                turned = rot * ext[(1 - comp) * total + p]
                moved = still[p] * value + spin * around + mixed[p] * sum(near[1:], near[0]) + force[comp * total + p]
                after.append(moved + turned if comp == 0 else moved - turned)
        if step < ITERS - 1:
            for comp in range(2):
                for p in range(needed):
                    ext[comp * total + p] = after[comp * needed + p]
        else:
            for comp in range(2):
                for level in range(z.levels):
                    place = level + sec * (z.levels - 1 - 2 * level)
                    currents_out[comp, place] = after[comp * needed + level][:ROWS, :LANES]


def tables(directions):
    quarter = directions // 4
    heading = (np.arange(quarter) + 0.5) * (2.0 * math.pi / directions)
    return np.stack([np.cos(heading), np.sin(heading)]).astype(np.float32)


def shifted(value, axis, steps):
    count = lax.axis_size(axis)
    return lax.ppermute(value, axis, [(i, (i + steps) % count) for i in range(count)])


def swapped(value, parity):
    lat, lon = lax.axis_size("lat"), lax.axis_size("lon")
    pairs = []
    for i in range(lat):
        other = i + 1 if i % 2 == parity else i - 1
        for j in range(lon):
            if 0 <= other < lat:
                pairs.append((i * lon + j, other * lon + j))
            elif j ^ 1 < lon:
                pairs.append((i * lon + j, i * lon + (j ^ 1)))
    return lax.ppermute(value, ("lat", "lon"), pairs)


def flat(tiles):
    return jax.ShapeDtypeStruct((tiles * ROWS, LANES), F32)


def stack(count):
    return jax.ShapeDtypeStruct((count, ROWS, LANES), F32)


def call(kernel, out_shape, in_specs, out_specs=None, scratch=(), name=None, bytes_accessed=0, flops=0):
    return pl.pallas_call(
        kernel,
        out_shape=out_shape,
        in_specs=in_specs,
        out_specs=out_specs if out_specs is not None else [VMEM] * len(out_shape),
        scratch_shapes=list(scratch),
        name=name,
        compiler_params=pltpu.CompilerParams(vmem_limit_bytes=24 * 1024 * 1024),
        cost_estimate=pl.CostEstimate(flops=flops, bytes_accessed=bytes_accessed, transcendentals=0),
    )


def shards(spectra, currents, land_mask, diffusion, courant, stokes_weight, stress_weight):
    freqs, directions, tile_rows, tile_cols = spectra.shape
    levels = currents.shape[1]
    lat_count = lax.axis_size("lat")
    assert lax.axis_size("sec") == 2 and (tile_rows, tile_cols) == (ROWS, LANES) and directions % 4 == 0
    z = Sizes(freqs, directions, levels)
    size = spectra.size * 4
    copies = 4 * len(chunks(z))
    sems = pltpu.SemaphoreType.DMA((copies,))
    whole = pltpu.VMEM(spectra.shape, F32)

    edge_rows = jax.ShapeDtypeStruct((z.edge_rows, LANES), F32)
    inputs = (spectra, currents, land_mask, diffusion, courant, stokes_weight, stress_weight)
    kept, pay, ecol, wcol, local, coef = call(
        functools.partial(sums_kernel, z),
        (
            whole,
            flat(z.sec_tiles),
            flat(z.col_tiles),
            flat(z.col_tiles),
            flat(2),
            flat(z.coef_tiles),
        ),
        [ANY] * 7,
        scratch=[
            pltpu.VMEM(currents.shape, F32),
            pltpu.VMEM(land_mask.shape, jnp.int32),
            pltpu.SMEM(courant.shape, F32),
            pltpu.SMEM(courant.shape, F32),
            pltpu.SMEM(courant.shape, F32),
            pltpu.VMEM((5 * SUMS, ROWS, LANES), F32),
            sems,
            pltpu.SemaphoreType.DMA((6,)),
        ],
        name="spectra_sums",
        bytes_accessed=size,
        flops=16 * size // 4,
    )(*[pltpu.with_memory_space_constraint(array, pltpu.HBM) for array in inputs])

    other = shifted(pay, "sec", 1)

    first_rows, second_rows = call(
        functools.partial(edge_rows_kernel, z),
        (edge_rows, edge_rows),
        [VMEM],
        name="pick_rows",
        bytes_accessed=size,
        flops=8 * size // 4,
    )(kept)

    got_first = swapped(first_rows, 0)
    got_second = swapped(second_rows, 1)

    picks, beside = call(
        functools.partial(matrices_kernel, z),
        (jax.ShapeDtypeStruct((z.half * ROWS, LANES), BF16), jax.ShapeDtypeStruct((2 * LANES, 2 * LANES), BF16)),
        [VMEM],
        name="matrices",
        bytes_accessed=size,
        flops=8388608,
    )(kept)

    fields, coup, flux, to_east, to_west = call(
        functools.partial(columns_kernel, z),
        (stack(z.fields), stack(4), flat(1 + z.sec_tiles - z.sec_rows), flat(1 + z.col_tiles), flat(1 + z.col_tiles)),
        [VMEM] * 6,
        name="pack_columns",
        bytes_accessed=2**18,
        flops=65536,
    )(pay, other, picks, local, ecol, wcol)

    from_east = shifted(to_west, "lon", -1)
    from_west = shifted(to_east, "lon", 1)

    coup, edges, to_first, to_second = call(
        functools.partial(rows_kernel, z),
        (stack(4), stack(z.arrays + SUMS), flat(z.lat_tiles), flat(z.lat_tiles)),
        [VMEM] * 6,
        name="pack_rows",
        bytes_accessed=2**18,
        flops=2**27,
    )(from_west, from_east, fields, coup, flux, local)

    from_second = swapped(to_second, 1)
    from_first = swapped(to_first, 0)

    new_spectra, coup = call(
        functools.partial(wave_kernel, z, lat_count),
        (jax.ShapeDtypeStruct(spectra.shape, F32), stack(4)),
        [VMEM] * 10,
        out_specs=[ANY, VMEM],
        scratch=[whole, pltpu.VMEM((directions, ROWS, LANES), F32), pltpu.VMEM((2, z.edge_rows, LANES), F32), sems],
        name="wave_step",
        bytes_accessed=2 * size,
        flops=8388608,
    )(kept, fields, coup, local, coef, picks, from_west, from_east, got_first, got_second)

    (new_currents,) = call(
        functools.partial(ocean_kernel, z, lat_count),
        (jax.ShapeDtypeStruct(currents.shape, F32),),
        [VMEM] * 8,
        scratch=[pltpu.VMEM((count, 2 * ROWS, 2 * LANES), F32) for count in (z.fields, z.fields, 2 * levels, 2 * levels)],
        name="ocean_steps",
        bytes_accessed=2**20,
        flops=2**20,
    )(from_first, from_second, fields, coup, flux, edges, local, beside)
    return new_spectra, new_currents


def solution(mesh):
    in_specs = (
        P("sec", None, "lat", "lon"),
        P(None, "sec", "lat", "lon"),
        P("lat", "lon"),
        P("lat", "lon"),
        P("sec"),
        P("sec"),
        P("sec"),
    )
    out_specs = (P("sec", None, "lat", "lon"), P(None, "sec", "lat", "lon"))
    return jax.shard_map(shards, mesh=mesh, in_specs=in_specs, out_specs=out_specs, check_vma=False)
```

```python
import functools
import math

import jax
import jax.numpy as jnp
import numpy as np
from jax import lax
from jax.experimental import pallas as pl
from jax.experimental.pallas import tpu as pltpu
from jax.sharding import PartitionSpec as P

ITERS = 4
ROWS = 8
LANES = 128
HALO = 4
MOMENTS = 5
SUMS = 2 * MOMENTS
FLUX_COLS = 3
current_gain = 0.1
stress_gain = 0.5

VMEM = pl.BlockSpec(memory_space=pltpu.VMEM)
SMEM = pl.BlockSpec(memory_space=pltpu.SMEM)
ANY = pl.BlockSpec(memory_space=pl.ANY)
F32 = jnp.float32
BF16 = jnp.bfloat16


def lanes():
    return lax.broadcasted_iota(jnp.int32, (ROWS, LANES), 1)


def rows():
    return lax.broadcasted_iota(jnp.int32, (ROWS, LANES), 0)


def lane_roll(tile, shift):
    if isinstance(shift, int):
        shift %= LANES
        if shift == 0:
            return tile
    return pltpu.roll(tile, shift, 1)


def row_roll(tile, shift):
    shift %= ROWS
    return tile if shift == 0 else pltpu.roll(tile, shift, 0)


def spread(ref, row):
    return jnp.broadcast_to(ref[pl.ds(row, 1), :], (ROWS, LANES))


def put(ref, index, tile):
    ref[pl.ds(index * ROWS, ROWS), :] = tile


def take(ref, index):
    return ref[pl.ds(index * ROWS, ROWS), :]


def coupled(sums, zonal, meridional, sea):
    result = []
    for w in range(2):
        c, s, cc, cs, ss = sums[w * MOMENTS : (w + 1) * MOMENTS]
        result.append(sea * (c + current_gain * (zonal * cc + meridional * cs)))
        result.append(sea * (s + current_gain * (zonal * cs + meridional * ss)))
    return result


class Sizes:
    def __init__(self, freqs, directions, levels):
        self.freqs = freqs
        self.directions = directions
        self.levels = levels
        self.quarter = directions // 4
        self.fields = 2 * 2 * levels
        self.half = directions // 2
        self.per_tile = LANES // self.half
        self.col_tiles = -(-freqs // self.per_tile)
        self.edge_rows = freqs * directions // 2
        self.sec_sums = self.fields // 2
        self.sec_cols = self.sec_sums + SUMS
        self.sec_rows = self.sec_cols + 1
        self.sec_tiles = self.sec_rows + -(-2 * SUMS // ROWS)
        self.lon_coup = HALO * (self.fields + 2)
        self.lon_flux = self.lon_coup + 4 * HALO
        self.lon_rows = self.lon_flux + SUMS
        self.arrays = self.fields + 2 + 4
        self.pairs = self.arrays // 2
        self.flux_tiles = -(-SUMS // ROWS)
        self.lat_pairs = 0
        self.lat_flux = self.lat_pairs + self.pairs
        self.lat_edges = self.lat_flux + self.flux_tiles
        self.lat_tiles = self.lat_edges + 1
        self.coef_tiles = -(-freqs // ROWS)
        assert self.lon_rows + SUMS * FLUX_COLS <= LANES
        assert (self.pairs + self.flux_tiles) * 2 * HALO <= LANES

    def headings(self, i):
        q = self.quarter
        return (i, 2 * q - 1 - i, 2 * q + i, 4 * q - 1 - i)


def chunks(z):
    q = z.quarter
    cuts = sorted({0, q * 4 // 9, q * 7 // 9, q})
    result = []
    for lo, hi in zip(cuts, cuts[1:]):
        starts = (lo, 2 * q - hi, 2 * q + lo, 4 * q - hi)
        result.append((lo, hi, [pl.ds(start, hi - lo) for start in starts]))
    return result


def sums_kernel(z, x, cur_in, mask_in, diffusion_in, courant_in, stokes_in, stress_in, buf, pay, ecol, wcol, local, coef, cur, mask, courant, stokes, stress, acc, sems, small_sems):
    q, nf = z.quarter, z.freqs
    pairs = ((cur_in, cur), (mask_in, mask), (diffusion_in, local.at[pl.ds(ROWS, ROWS)]), (courant_in, courant), (stokes_in, stokes), (stress_in, stress))
    small = [pltpu.make_async_copy(source, target, small_sems.at[k]) for k, (source, target) in enumerate(pairs)]
    for copy in small:
        copy.start()
    copies = []
    for g, (_, _, spans) in enumerate(chunks(z)):
        for j, span in enumerate(spans):
            copies.append(pltpu.make_async_copy(x.at[:, span], buf.at[:, span], sems.at[4 * g + j]))
    for copy in copies:
        copy.start()

    lane, row = lanes(), rows()
    zero = jnp.zeros((ROWS, LANES), F32)
    for k in range(5 * SUMS):
        acc[k] = zero
    sizes = tables(z.directions)
    east, west = [zero] * z.col_tiles, [zero] * z.col_tiles
    for copy in small:
        copy.wait()
    sea = mask[...].astype(F32)
    put(local, 0, sea)
    for comp in range(2):
        for level in range(z.levels):
            put(pay, comp * z.levels + level, cur[comp, level] * sea)
    for f in range(nf):
        coef[pl.ds(f, 1), :] = jnp.full((1, LANES), courant[f], F32)

    def add(i):
        c, s = float(sizes[0, i]), float(sizes[1, i])
        heading = z.headings(i)
        total = [[zero] * 4 for _ in range(4)]
        for f in range(nf):
            t = f // z.per_tile
            cg = courant[f]
            factors = (stokes[f], stokes[f] * cg, stress[f], stress[f] * cg)
            for j in range(4):
                energy = buf[f, heading[j]]
                for k in range(4):
                    total[k][j] = total[k][j] + factors[k] * energy
                at = f % z.per_tile * z.half + 2 * i + (0 if j in (0, 1) else 1)
                if j in (0, 3):
                    east[t] = jnp.where(lane == at, lane_roll(energy, at - (LANES - 1)), east[t])
                else:
                    west[t] = jnp.where(lane == at, lane_roll(energy, at), west[t])
        cc, cs, ss = c * c, c * s, s * s
        for w in range(2):
            plain, fast = total[2 * w], total[2 * w + 1]
            both = c + s
            h = [plain[j] - both * fast[j] for j in range(4)]
            here, there = h[0] + h[3], h[1] + h[2]
            every = here + there
            values = [
                c * (here - there),
                s * ((h[0] + h[1]) - (h[2] + h[3])),
                cc * every,
                cs * ((h[0] - h[3]) + (h[2] - h[1])),
                ss * every,
            ]
            for a, b, size, signs in (
                (fast[0] + fast[3], fast[0] - fast[3], c, (1, 1, 1)),
                (fast[1] + fast[2], fast[1] - fast[2], c, (-1, 1, -1)),
            ):
                values += [signs[0] * size * c * a, signs[1] * size * s * b, size * cc * a, signs[2] * size * cs * b, size * ss * a]
            for a, b, size, signs in (
                (fast[0] + fast[1], fast[0] - fast[1], s, (1, 1, 1)),
                (fast[2] + fast[3], fast[3] - fast[2], s, (1, -1, -1)),
            ):
                values += [signs[0] * size * c * b, signs[1] * size * s * a, size * cc * a, signs[2] * size * cs * b, size * ss * a]
            for kind in range(5):
                for m in range(MOMENTS):
                    at = kind * SUMS + w * MOMENTS + m
                    acc[at] = acc[at] + values[kind * MOMENTS + m]

    for g, (lo, hi, _) in enumerate(chunks(z)):
        for copy in copies[4 * g : 4 * g + 4]:
            copy.wait()
        for i in range(lo, hi):
            add(i)
    for t in range(z.col_tiles):
        put(ecol, t, east[t])
        put(wcol, t, west[t])

    cols = zero
    for k in range(SUMS):
        center, east, west, north, south = (acc[kind * SUMS + k] for kind in range(5))
        value = center + jnp.where(lane > 0, lane_roll(east, 1), 0.0) + jnp.where(lane < LANES - 1, lane_roll(west, -1), 0.0)
        value = value + jnp.where(row > 0, row_roll(north, 1), 0.0) + jnp.where(row < ROWS - 1, row_roll(south, -1), 0.0)
        put(pay, z.sec_sums + k, value)
        cols = jnp.where(lane == k, lane_roll(east, k - (LANES - 1)), cols)
        cols = jnp.where(lane == SUMS + k, lane_roll(west, SUMS + k), cols)
        pay[pl.ds(z.sec_rows * ROWS + k, 1), :] = north[ROWS - 1 :]
        pay[pl.ds(z.sec_rows * ROWS + SUMS + k, 1), :] = south[:1]
    put(pay, z.sec_cols, cols)
    spare = (z.sec_tiles - z.sec_rows) * ROWS - 2 * SUMS
    if spare:
        pay[pl.ds(z.sec_tiles * ROWS - spare, spare), :] = jnp.zeros((spare, LANES), F32)


def parts(tile):
    high = tile.astype(BF16).astype(F32)
    return high, (tile - high).astype(BF16).astype(F32)


def edge_rows_kernel(z, turn, x, out):
    flat = x.reshape(z.freqs * z.directions * ROWS, LANES)
    north, south = ROWS - 1, z.half * ROWS
    start = jnp.where(lax.rem(lax.axis_index("lat"), 2) == turn, north, south)
    for f in range(z.freqs):
        out[pl.ds(f * z.half, z.half), :] = flat[pl.ds(f * z.directions * ROWS + start, z.half, stride=ROWS), :]


def picks_kernel(z, x, picks):
    lane = lanes()
    for k in range(z.half // 2):
        both = [((lane & (LANES // 2 - 1)) == 2 * k + n).astype(F32) for n in range(2)]
        picks[pl.ds(2 * ROWS * k, 2 * ROWS), :] = jnp.concatenate(both, axis=0).astype(BF16)


def columns_kernel(z, mine, other, picks, local, ecol, wcol, fields, coup, flux, to_east, to_west):
    lane, row = lanes(), rows()
    sec = lax.axis_index("sec")
    total = 2 * z.levels
    for comp in range(2):
        for level in range(z.levels):
            own = level + sec * (z.levels - 1 - 2 * level)
            far = z.levels + level + sec * (z.levels - 1 - 2 * level)
            fields[comp * total + own] = take(mine, comp * z.levels + level)
            fields[comp * total + far] = take(other, comp * z.levels + level)
    sea, diffusion = take(local, 0), take(local, 1)
    top = sec * (total - 1)
    zonal, meridional = fields[top], fields[total + top]
    sums = [take(mine, z.sec_sums + k) + take(other, z.sec_sums + k) for k in range(SUMS)]
    coupling = coupled(sums, zonal, meridional, sea)
    cols = take(mine, z.sec_cols) + take(other, z.sec_cols)
    put(flux, 0, cols)
    for t in range(z.sec_tiles - z.sec_rows):
        put(flux, 1 + t, take(mine, z.sec_rows + t) + take(other, z.sec_rows + t))
    for k in range(4):
        coup[k] = coupling[k]
    arrays = [fields[k] for k in range(z.fields)] + [sea, diffusion] + coupling
    east, west = lane_roll(cols, z.lon_flux), lane_roll(cols, z.lon_flux - SUMS)
    for k, array in enumerate(arrays):
        mine_here = (lane >= HALO * k) & (lane < HALO * (k + 1))
        east = jnp.where(mine_here, lane_roll(array, HALO * (k + 1)), east)
        west = jnp.where(mine_here, lane_roll(array, HALO * k), west)
    for k in range(SUMS):
        edge = jnp.where(row == ROWS - 1, spread(flux, ROWS + k), spread(flux, ROWS + SUMS + k))
        at = z.lon_rows + FLUX_COLS * k
        mine_here = (lane >= at) & (lane < at + FLUX_COLS)
        east = jnp.where(mine_here, lane_roll(edge, at + FLUX_COLS), east)
        west = jnp.where(mine_here, lane_roll(edge, at), west)
    put(to_east, 0, east)
    put(to_west, 0, west)
    for t in range(z.col_tiles):
        put(to_east, 1 + t, take(ecol, t))
        put(to_west, 1 + t, take(wcol, t))


def rows_kernel(z, from_east, from_west, fields, coup, flux, local, got_rows, coup_out, edges, to_first, to_second):
    lane, row = lanes(), rows()
    total = 2 * z.levels
    top = lax.axis_index("sec") * (total - 1)
    sea, diffusion = take(local, 0), take(local, 1)
    cols = take(flux, 0)
    west, east = take(from_west, 0), take(from_east, 0)

    def beyond(first, width):
        near = lane_roll(east, -first)
        far = lane_roll(west, LANES - width - first)
        return jnp.where(lane < width, near, jnp.where(lane >= LANES - width, far, 0.0))

    edge = [beyond(HALO * k, HALO) for k in range(z.fields + 2)]
    for k in range(z.fields + 2):
        edges[k] = edge[k]
    inner, outer = [], []
    for k in range(SUMS):
        at = z.lon_flux + k
        inner.append(jnp.where(lane == 0, lane_roll(west, -at), jnp.where(lane == LANES - 1, lane_roll(east, LANES - 1 - at), 0.0)))
        outer.append(jnp.where(lane == 0, lane_roll(cols, -k), jnp.where(lane == LANES - 1, lane_roll(cols, LANES - 1 - SUMS - k), 0.0)))
    inside = coupled(inner, fields[top], fields[total + top], sea)
    outside = coupled(outer, edges[top], edges[total + top], edge[z.fields])
    main_coupling = [coup[k] + inside[k] for k in range(4)]
    edge_coupling = [beyond(z.lon_coup + HALO * k, HALO) + outside[k] for k in range(4)]
    for k in range(4):
        coup_out[k] = main_coupling[k]
        edges[z.fields + 2 + k] = edge_coupling[k]
    row_edge = [beyond(z.lon_rows + FLUX_COLS * k, FLUX_COLS) for k in range(SUMS)]
    for k in range(SUMS):
        edges[z.arrays + k] = row_edge[k]

    main = [fields[k] for k in range(z.fields)] + [sea, diffusion] + main_coupling
    edge = edge + edge_coupling
    low = row < HALO
    odd = lax.rem(lax.axis_index("lat"), 2) == 1

    def send(index, north, south):
        put(to_first, index, jnp.where(odd, south, north))
        put(to_second, index, jnp.where(odd, north, south))

    def pair(a, b):
        return jnp.where(low, row_roll(b, HALO), a), jnp.where(low, a, row_roll(b, HALO))

    def group(tile, k):
        at = 2 * HALO * k
        in_group = lax.rem(lane + LANES + HALO - at, LANES) < 2 * HALO
        return in_group, lane_roll(tile, at)

    north_edges = jnp.zeros((ROWS, LANES), F32)
    south_edges = north_edges
    for k in range(z.pairs):
        north, south = pair(main[2 * k], main[2 * k + 1])
        send(z.lat_pairs + k, north, south)
        north, south = pair(edge[2 * k], edge[2 * k + 1])
        in_group, moved = group(north, k)
        north_edges = jnp.where(in_group, moved, north_edges)
        in_group, moved = group(south, k)
        south_edges = jnp.where(in_group, moved, south_edges)
    for t in range(z.flux_tiles):
        north, south = jnp.zeros((ROWS, LANES), F32), jnp.zeros((ROWS, LANES), F32)
        north_row, south_row = north, south
        for r in range(min(ROWS, SUMS - t * ROWS)):
            k = t * ROWS + r
            north = jnp.where(row == r, spread(flux, ROWS + k), north)
            south = jnp.where(row == r, spread(flux, ROWS + SUMS + k), south)
            north_row = jnp.where(row == r, jnp.broadcast_to(row_edge[k][ROWS - 1 :], (ROWS, LANES)), north_row)
            south_row = jnp.where(row == r, jnp.broadcast_to(row_edge[k][:1], (ROWS, LANES)), south_row)
        send(z.lat_flux + t, north, south)
        in_group, moved = group(north_row, z.pairs + t)
        north_edges = jnp.where(in_group, moved, north_edges)
        in_group, moved = group(south_row, z.pairs + t)
        south_edges = jnp.where(in_group, moved, south_edges)
    send(z.lat_edges, north_edges, south_edges)


def side_signs(j):
    return (1 if j in (0, 3) else -1), (1 if j in (0, 1) else -1)


def lat_sides(first, second, lat_count):
    place = lax.axis_index("lat")
    odd = lax.rem(place, 2) == 1
    north = jnp.where(place < lat_count - 1, jnp.where(odd, second, first), 0.0)
    south = jnp.where(place > 0, jnp.where(odd, first, second), 0.0)
    return north, south


def wave_kernel(z, lat_count, x, fields, coup, local, coef, picks, from_west, from_east, first, second, out, coup_out, buf, scales, sides, sems):
    q, nf, half = z.quarter, z.freqs, z.half
    lane, row = lanes(), rows()
    total = 2 * z.levels
    top = lax.axis_index("sec") * (total - 1)
    sea = take(local, 0)
    zonal, meridional = current_gain * fields[top], current_gain * fields[total + top]
    coup_out[...] = coup[...]
    sides[0], sides[1] = lat_sides(first[...], second[...], lat_count)
    sizes = tables(z.directions)
    headings = []
    for i in range(q):
        c, s = float(sizes[0, i]), float(sizes[1, i])
        for j, heading in enumerate(z.headings(i)):
            sign_x, sign_y = side_signs(j)
            headings.append((heading, i, sign_x, sign_y, 2 * i + (0 if j in (0, 1) else 1)))
            scales[heading] = sea * (1.0 + (sign_x * c) * zonal + (sign_y * s) * meridional)
    ones = jnp.ones((LANES, LANES), BF16)

    def body(f, _):
        speed = spread(coef, f)
        along = [speed * float(sizes[0, i]) for i in range(q)]
        across = [speed * float(sizes[1, i]) for i in range(q)]
        stay = [1.0 - along[i] - across[i] for i in range(q)]
        at = pl.ds(pl.multiple_of((1 + (f // z.per_tile)) * ROWS, ROWS), ROWS)
        back = LANES - half * (f % z.per_tile)
        rims = []
        for ref in (from_west, from_east):
            high, low = parts(lane_roll(ref[at, :], back))
            both = jnp.where(lane < LANES // 2, high, lane_roll(low, LANES // 2))
            both = jnp.concatenate([both, both], axis=0).astype(BF16)
            chosen = jnp.concatenate([both] * (half // 2), axis=0) * picks[...]
            rims.append(jnp.dot(chosen, ones, preferred_element_type=F32))
        for heading, i, sign_x, sign_y, k in headings:
            energy = x[f, heading]
            if sign_x > 0:
                beside = jnp.where(lane == 0, rims[0][k * ROWS : (k + 1) * ROWS], lane_roll(energy, 1))
            else:
                beside = jnp.where(lane == LANES - 1, rims[1][k * ROWS : (k + 1) * ROWS], lane_roll(energy, -1))
            if sign_y > 0:
                below = jnp.where(row == 0, spread(sides.at[1], f * half + heading), row_roll(energy, 1))
            else:
                below = jnp.where(row == ROWS - 1, spread(sides.at[0], f * half + heading - half), row_roll(energy, -1))
            buf[f, heading] = scales[heading] * (stay[i] * energy + along[i] * beside + across[i] * below)
        return 0

    count = 6 if nf % 6 == 0 else 1
    copies = []
    for g in range(count):
        span = pl.ds(g * (nf // count), nf // count)
        lax.fori_loop(g * (nf // count), (g + 1) * (nf // count), body, 0, unroll=3 if nf % 18 == 0 else 1)
        copy = pltpu.make_async_copy(buf.at[span], out.at[span], sems.at[g])
        copy.start()
        copies.append(copy)
    for copy in copies:
        copy.wait()


def ocean_kernel(z, lat_count, from_first, from_second, fields, coup, flux, edges, local, currents_out, ext, force, still, mixed):
    total = 2 * z.levels
    row = rows()
    sec = lax.axis_index("sec")
    top = sec * (total - 1)
    sea, diffusion = take(local, 0), take(local, 1)
    low = row < HALO

    def pair(north, south):
        first = jnp.where(low, north, south)
        second = jnp.where(low, row_roll(north, HALO), row_roll(south, HALO))
        return first, second

    def sides(index):
        return lat_sides(take(from_first, index), take(from_second, index), lat_count)

    north_edges, south_edges = sides(z.lat_edges)
    north_rows, south_rows = zip(*[sides(z.lat_flux + t) for t in range(z.flux_tiles)])
    halo, halo_edge = [], []
    for k in range(z.pairs):
        halo += pair(*sides(z.lat_pairs + k))
        halo_edge += pair(lane_roll(north_edges, -2 * HALO * k), lane_roll(south_edges, -2 * HALO * k))
    inner, outer, inner_edge, outer_edge = [], [], [], []
    for k in range(SUMS):
        t, r = k // ROWS, k % ROWS
        high = row == ROWS - 1
        bottom = row == 0
        north = jnp.broadcast_to(north_rows[t][r : r + 1], (ROWS, LANES))
        south = jnp.broadcast_to(south_rows[t][r : r + 1], (ROWS, LANES))
        inner.append(jnp.where(high, north, jnp.where(bottom, south, 0.0)))
        outer.append(jnp.where(bottom, spread(flux, ROWS + k), jnp.where(high, spread(flux, ROWS + SUMS + k), 0.0)))
        shift = -2 * HALO * (z.pairs + t)
        north = jnp.broadcast_to(lane_roll(north_edges, shift)[r : r + 1], (ROWS, LANES))
        south = jnp.broadcast_to(lane_roll(south_edges, shift)[r : r + 1], (ROWS, LANES))
        inner_edge.append(jnp.where(high, north, jnp.where(bottom, south, 0.0)))
        mine = edges[z.arrays + k]
        outer_edge.append(
            jnp.where(bottom, jnp.broadcast_to(mine[ROWS - 1 :], (ROWS, LANES)), jnp.where(high, jnp.broadcast_to(mine[:1], (ROWS, LANES)), 0.0))
        )

    def joined(main, edge, halo_main, halo_side):
        return jnp.concatenate([jnp.concatenate([main, edge], axis=1), jnp.concatenate([halo_main, halo_side], axis=1)], axis=0)

    for k in range(z.fields):
        ext[k] = joined(fields[k], edges[k], halo[k], halo_edge[k])
    sea_all = joined(sea, edges[z.fields], halo[z.fields], halo_edge[z.fields])
    kappa = joined(diffusion, edges[z.fields + 1], halo[z.fields + 1], halo_edge[z.fields + 1])
    sums = [joined(inner[k], inner_edge[k], outer[k], outer_edge[k]) for k in range(SUMS)]
    extra = coupled(sums, ext[top], ext[total + top], sea_all)
    first = z.fields + 2
    coupling = [joined(coup[k], edges[first + k], halo[first + k], halo_edge[first + k]) + extra[k] for k in range(4)]

    shape = (2 * ROWS, 2 * LANES)
    row_all = lax.broadcasted_iota(jnp.int32, shape, 0)
    row_all = jnp.where(row_all >= 2 * ROWS - HALO, row_all - 2 * ROWS, row_all) + lax.axis_index("lat") * ROWS
    rot = sea_all * (0.05 + 0.1 * (row_all.astype(F32) + 0.5) * (1.0 / (lat_count * ROWS)))
    spin = sea_all * kappa

    def by_level(function, p):
        return jnp.where(sec == 0, function(p), function(total - 1 - p)).astype(F32)

    for p in range(total):
        mix, decay, gain = by_level(lambda level: 0.04 + 0.0125 * (7 * level % 5), p), by_level(lambda level: 1.0 / (1.0 + level), p), by_level(lambda level: stress_gain if level == 0 else 0.0, p)
        force[p] = rot * decay * coupling[1] + sea_all * gain * coupling[2]
        force[total + p] = sea_all * gain * coupling[3] - rot * decay * coupling[0]
        mixed[p] = sea_all * mix
        still[p] = sea_all * (1.0 - mix * (1 if p in (0, total - 1) else 2)) - 4.0 * spin
    for step in range(ITERS):
        needed = min(total, z.levels + ITERS - 1 - step)
        every = [ext[comp * total + p] for comp in range(2) for p in range(needed)]
        after = []
        for comp in range(2):
            for p in range(needed):
                at = comp * needed + p
                value = every[at]
                around = (pltpu.roll(value, 1, 1) + pltpu.roll(value, 2 * LANES - 1, 1)) + (pltpu.roll(value, 1, 0) + pltpu.roll(value, 2 * ROWS - 1, 0))
                near = [ext[comp * total + other] for other in (p - 1, p + 1) if 0 <= other < total]
                turned = rot * ext[(1 - comp) * total + p]
                moved = still[p] * value + spin * around + mixed[p] * sum(near[1:], near[0]) + force[comp * total + p]
                after.append(moved + turned if comp == 0 else moved - turned)
        if step < ITERS - 1:
            for comp in range(2):
                for p in range(needed):
                    ext[comp * total + p] = after[comp * needed + p]
        else:
            for comp in range(2):
                for level in range(z.levels):
                    place = level + sec * (z.levels - 1 - 2 * level)
                    currents_out[comp, place] = after[comp * needed + level][:ROWS, :LANES]


def tables(directions):
    quarter = directions // 4
    heading = (np.arange(quarter) + 0.5) * (2.0 * math.pi / directions)
    return np.stack([np.cos(heading), np.sin(heading)]).astype(np.float32)


def shifted(value, axis, steps):
    count = lax.axis_size(axis)
    return lax.ppermute(value, axis, [(i, (i + steps) % count) for i in range(count)])


def swapped(value, parity):
    lat, lon = lax.axis_size("lat"), lax.axis_size("lon")
    pairs = []
    for i in range(lat):
        other = i + 1 if i % 2 == parity else i - 1
        for j in range(lon):
            if 0 <= other < lat:
                pairs.append((i * lon + j, other * lon + j))
            elif j ^ 1 < lon:
                pairs.append((i * lon + j, i * lon + (j ^ 1)))
    return lax.ppermute(value, ("lat", "lon"), pairs)


def flat(tiles):
    return jax.ShapeDtypeStruct((tiles * ROWS, LANES), F32)


def stack(count):
    return jax.ShapeDtypeStruct((count, ROWS, LANES), F32)


def call(kernel, out_shape, in_specs, out_specs=None, scratch=(), name=None, bytes_accessed=0, flops=0):
    return pl.pallas_call(
        kernel,
        out_shape=out_shape,
        in_specs=in_specs,
        out_specs=out_specs if out_specs is not None else [VMEM] * len(out_shape),
        scratch_shapes=list(scratch),
        name=name,
        compiler_params=pltpu.CompilerParams(vmem_limit_bytes=24 * 1024 * 1024),
        cost_estimate=pl.CostEstimate(flops=flops, bytes_accessed=bytes_accessed, transcendentals=0),
    )


def shards(spectra, currents, land_mask, diffusion, courant, stokes_weight, stress_weight):
    freqs, directions, tile_rows, tile_cols = spectra.shape
    levels = currents.shape[1]
    lat_count = lax.axis_size("lat")
    assert lax.axis_size("sec") == 2 and (tile_rows, tile_cols) == (ROWS, LANES) and directions % 4 == 0
    z = Sizes(freqs, directions, levels)
    size = spectra.size * 4
    copies = 4 * len(chunks(z))
    sems = pltpu.SemaphoreType.DMA((copies,))
    whole = pltpu.VMEM(spectra.shape, F32)

    edge_rows = jax.ShapeDtypeStruct((z.edge_rows, LANES), F32)
    inputs = (spectra, currents, land_mask, diffusion, courant, stokes_weight, stress_weight)
    kept, pay, ecol, wcol, local, coef = call(
        functools.partial(sums_kernel, z),
        (
            whole,
            flat(z.sec_tiles),
            flat(z.col_tiles),
            flat(z.col_tiles),
            flat(2),
            flat(z.coef_tiles),
        ),
        [ANY] * 7,
        scratch=[
            pltpu.VMEM(currents.shape, F32),
            pltpu.VMEM(land_mask.shape, jnp.int32),
            pltpu.SMEM(courant.shape, F32),
            pltpu.SMEM(courant.shape, F32),
            pltpu.SMEM(courant.shape, F32),
            pltpu.VMEM((5 * SUMS, ROWS, LANES), F32),
            sems,
            pltpu.SemaphoreType.DMA((6,)),
        ],
        name="spectra_sums",
        bytes_accessed=size,
        flops=16 * size // 4,
    )(*[pltpu.with_memory_space_constraint(array, pltpu.HBM) for array in inputs])

    other = shifted(pay, "sec", 1)

    got_first, got_second = [
        swapped(
            call(
                functools.partial(edge_rows_kernel, z, turn),
                (edge_rows,),
                [VMEM],
                name="pick_rows",
                bytes_accessed=size // 16,
                flops=2**16,
            )(kept)[0],
            turn,
        )
        for turn in range(2)
    ]

    (picks,) = call(
        functools.partial(picks_kernel, z),
        (jax.ShapeDtypeStruct((z.half * ROWS, LANES), BF16),),
        [VMEM],
        name="picks",
        bytes_accessed=size,
        flops=8388608,
    )(kept)

    fields, coup, flux, to_east, to_west = call(
        functools.partial(columns_kernel, z),
        (stack(z.fields), stack(4), flat(1 + z.sec_tiles - z.sec_rows), flat(1 + z.col_tiles), flat(1 + z.col_tiles)),
        [VMEM] * 6,
        name="pack_columns",
        bytes_accessed=2**18,
        flops=1073741824,
    )(pay, other, picks, local, ecol, wcol)

    from_east = shifted(to_west, "lon", -1)
    from_west = shifted(to_east, "lon", 1)

    coup, edges, to_first, to_second = call(
        functools.partial(rows_kernel, z),
        (stack(4), stack(z.arrays + SUMS), flat(z.lat_tiles), flat(z.lat_tiles)),
        [VMEM] * 7,
        name="pack_rows",
        bytes_accessed=2**18,
        flops=2**27,
    )(from_east, from_west, fields, coup, flux, local, got_second)

    from_second = swapped(to_second, 1)
    from_first = swapped(to_first, 0)

    new_spectra, coup = call(
        functools.partial(wave_kernel, z, lat_count),
        (jax.ShapeDtypeStruct(spectra.shape, F32), stack(4)),
        [VMEM] * 10,
        out_specs=[ANY, VMEM],
        scratch=[whole, pltpu.VMEM((directions, ROWS, LANES), F32), pltpu.VMEM((2, z.edge_rows, LANES), F32), sems],
        name="wave_step",
        bytes_accessed=2 * size,
        flops=9 * size // 4,
    )(kept, fields, coup, local, coef, picks, from_west, from_east, got_first, got_second)

    (new_currents,) = call(
        functools.partial(ocean_kernel, z, lat_count),
        (jax.ShapeDtypeStruct(currents.shape, F32),),
        [VMEM] * 7,
        scratch=[pltpu.VMEM((count, 2 * ROWS, 2 * LANES), F32) for count in (z.fields, z.fields, 2 * levels, 2 * levels)],
        name="ocean_steps",
        bytes_accessed=2**20,
        flops=2**20,
    )(from_first, from_second, fields, coup, flux, edges, local)
    return new_spectra, new_currents


def solution(mesh):
    in_specs = (
        P("sec", None, "lat", "lon"),
        P(None, "sec", "lat", "lon"),
        P("lat", "lon"),
        P("lat", "lon"),
        P("sec"),
        P("sec"),
        P("sec"),
    )
    out_specs = (P("sec", None, "lat", "lon"), P(None, "sec", "lat", "lon"))
    return jax.shard_map(shards, mesh=mesh, in_specs=in_specs, out_specs=out_specs, check_vma=False)
```

```python
import functools
import math

import jax
import jax.numpy as jnp
import numpy as np
from jax import lax
from jax.experimental import pallas as pl
from jax.experimental.pallas import tpu as pltpu
from jax.sharding import PartitionSpec as P

ITERS = 4
ROWS = 8
LANES = 128
HALO = 4
MOMENTS = 5
SUMS = 2 * MOMENTS
FLUX_COLS = 3
current_gain = 0.1
stress_gain = 0.5

VMEM = pl.BlockSpec(memory_space=pltpu.VMEM)
SMEM = pl.BlockSpec(memory_space=pltpu.SMEM)
ANY = pl.BlockSpec(memory_space=pl.ANY)
F32 = jnp.float32
BF16 = jnp.bfloat16


def lanes():
    return lax.broadcasted_iota(jnp.int32, (ROWS, LANES), 1)


def rows():
    return lax.broadcasted_iota(jnp.int32, (ROWS, LANES), 0)


def lane_roll(tile, shift):
    if isinstance(shift, int):
        shift %= LANES
        if shift == 0:
            return tile
    return pltpu.roll(tile, shift, 1)


def row_roll(tile, shift):
    shift %= ROWS
    return tile if shift == 0 else pltpu.roll(tile, shift, 0)


def spread(ref, row):
    return jnp.broadcast_to(ref[pl.ds(row, 1), :], (ROWS, LANES))


def put(ref, index, tile):
    ref[pl.ds(index * ROWS, ROWS), :] = tile


def take(ref, index):
    return ref[pl.ds(index * ROWS, ROWS), :]


def coupled(sums, zonal, meridional, sea):
    result = []
    for w in range(2):
        c, s, cc, cs, ss = sums[w * MOMENTS : (w + 1) * MOMENTS]
        result.append(sea * (c + current_gain * (zonal * cc + meridional * cs)))
        result.append(sea * (s + current_gain * (zonal * cs + meridional * ss)))
    return result


class Sizes:
    def __init__(self, freqs, directions, levels):
        self.freqs = freqs
        self.directions = directions
        self.levels = levels
        self.quarter = directions // 4
        self.fields = 2 * 2 * levels
        self.half = directions // 2
        self.per_tile = LANES // self.half
        self.col_tiles = -(-freqs // self.per_tile)
        self.edge_rows = -(-freqs * directions // 2 // ROWS) * ROWS
        assert self.half >= ROWS
        self.sec_sums = self.fields // 2
        self.sec_cols = self.sec_sums + SUMS
        self.sec_rows = self.sec_cols + 1
        self.sec_tiles = self.sec_rows + -(-2 * SUMS // ROWS)
        self.lon_coup = HALO * (self.fields + 2)
        self.lon_flux = self.lon_coup + 4 * HALO
        self.lon_rows = self.lon_flux + SUMS
        self.arrays = self.fields + 2 + 4
        self.pairs = self.arrays // 2
        self.flux_tiles = -(-SUMS // ROWS)
        self.lat_pairs = 0
        self.lat_flux = self.lat_pairs + self.pairs
        self.lat_edges = self.lat_flux + self.flux_tiles
        self.lat_tiles = self.lat_edges + 1
        self.coef_tiles = -(-freqs // ROWS)
        assert self.lon_rows + SUMS * FLUX_COLS <= LANES
        assert (self.pairs + self.flux_tiles) * 2 * HALO <= LANES

    def headings(self, i):
        q = self.quarter
        return (i, 2 * q - 1 - i, 2 * q + i, 4 * q - 1 - i)


def chunks(z):
    q = z.quarter
    cuts = sorted({0, q * 5 // 9, q})
    result = []
    for lo, hi in zip(cuts, cuts[1:]):
        starts = (lo, 2 * q - hi, 2 * q + lo, 4 * q - hi)
        result.append((lo, hi, [pl.ds(start, hi - lo) for start in starts]))
    return result


def sums_kernel(z, x, cur_in, mask_in, diffusion_in, courant_in, stokes_in, stress_in, buf, pay, ecol, wcol, local, coef, cur, mask, courant, stokes, stress, acc, sems, small_sems):
    q, nf = z.quarter, z.freqs
    pairs = ((cur_in, cur), (mask_in, mask), (diffusion_in, local.at[pl.ds(ROWS, ROWS)]), (courant_in, courant), (stokes_in, stokes), (stress_in, stress))
    small = [pltpu.make_async_copy(source, target, small_sems.at[k]) for k, (source, target) in enumerate(pairs)]
    for copy in small:
        copy.start()
    copies = []
    for g, (_, _, spans) in enumerate(chunks(z)):
        for j, span in enumerate(spans):
            copies.append(pltpu.make_async_copy(x.at[:, span], buf.at[:, span], sems.at[4 * g + j]))
    for copy in copies:
        copy.start()

    lane, row = lanes(), rows()
    zero = jnp.zeros((ROWS, LANES), F32)
    for k in range(5 * SUMS):
        acc[k] = zero
    sizes = tables(z.directions)
    east, west = [zero] * z.col_tiles, [zero] * z.col_tiles
    for copy in small:
        copy.wait()
    sea = mask[...].astype(F32)
    put(local, 0, sea)
    for comp in range(2):
        for level in range(z.levels):
            put(pay, comp * z.levels + level, cur[comp, level] * sea)
    for t in range(z.coef_tiles):
        tile = zero
        for f in range(t * ROWS, min(nf, (t + 1) * ROWS)):
            tile = jnp.where(row == f - t * ROWS, courant[f], tile)
        put(coef, t, tile)

    def add(i):
        c, s = float(sizes[0, i]), float(sizes[1, i])
        heading = z.headings(i)
        total = [[zero] * 4 for _ in range(4)]
        for f in range(nf):
            t = f // z.per_tile
            cg = courant[f]
            factors = (stokes[f], stokes[f] * cg, stress[f], stress[f] * cg)
            for j in range(4):
                energy = buf[f, heading[j]]
                for k in range(4):
                    total[k][j] = total[k][j] + factors[k] * energy
                at = f % z.per_tile * z.half + 2 * i + (0 if j in (0, 1) else 1)
                if j in (0, 3):
                    east[t] = jnp.where(lane == at, lane_roll(energy, at - (LANES - 1)), east[t])
                else:
                    west[t] = jnp.where(lane == at, lane_roll(energy, at), west[t])
        cc, cs, ss = c * c, c * s, s * s
        for w in range(2):
            plain, fast = total[2 * w], total[2 * w + 1]
            both = c + s
            h = [plain[j] - both * fast[j] for j in range(4)]
            here, there = h[0] + h[3], h[1] + h[2]
            every = here + there
            values = [
                c * (here - there),
                s * ((h[0] + h[1]) - (h[2] + h[3])),
                cc * every,
                cs * ((h[0] - h[3]) + (h[2] - h[1])),
                ss * every,
            ]
            for a, b, size, signs in (
                (fast[0] + fast[3], fast[0] - fast[3], c, (1, 1, 1)),
                (fast[1] + fast[2], fast[1] - fast[2], c, (-1, 1, -1)),
            ):
                values += [signs[0] * size * c * a, signs[1] * size * s * b, size * cc * a, signs[2] * size * cs * b, size * ss * a]
            for a, b, size, signs in (
                (fast[0] + fast[1], fast[0] - fast[1], s, (1, 1, 1)),
                (fast[2] + fast[3], fast[3] - fast[2], s, (1, -1, -1)),
            ):
                values += [signs[0] * size * c * b, signs[1] * size * s * a, size * cc * a, signs[2] * size * cs * b, size * ss * a]
            for kind in range(5):
                for m in range(MOMENTS):
                    at = kind * SUMS + w * MOMENTS + m
                    acc[at] = acc[at] + values[kind * MOMENTS + m]

    for g, (lo, hi, _) in enumerate(chunks(z)):
        for copy in copies[4 * g : 4 * g + 4]:
            copy.wait()
        for i in range(lo, hi):
            add(i)
    for t in range(z.col_tiles):
        put(ecol, t, east[t])
        put(wcol, t, west[t])

    cols = zero
    rims = [zero] * (z.sec_tiles - z.sec_rows)
    for k in range(SUMS):
        center, east, west, north, south = (acc[kind * SUMS + k] for kind in range(5))
        value = center + jnp.where(lane > 0, lane_roll(east, 1), 0.0) + jnp.where(lane < LANES - 1, lane_roll(west, -1), 0.0)
        value = value + jnp.where(row > 0, row_roll(north, 1), 0.0) + jnp.where(row < ROWS - 1, row_roll(south, -1), 0.0)
        put(pay, z.sec_sums + k, value)
        cols = jnp.where(lane == k, lane_roll(east, k - (LANES - 1)), cols)
        cols = jnp.where(lane == SUMS + k, lane_roll(west, SUMS + k), cols)
        for at, tile, edge in ((k, north, ROWS - 1), (SUMS + k, south, 0)):
            t, r = at // ROWS, at % ROWS
            rims[t] = jnp.where(row == r, row_roll(tile, r - edge), rims[t])
    put(pay, z.sec_cols, cols)
    for t, tile in enumerate(rims):
        put(pay, z.sec_rows + t, tile)


def parts(tile):
    high = tile.astype(BF16).astype(F32)
    return high, (tile - high).astype(BF16).astype(F32)


def edge_rows_kernel(z, turn, x, out):
    flat = x.reshape(z.freqs * z.directions * ROWS, LANES)
    north, south = ROWS - 1, z.half * ROWS
    start = jnp.where(lax.rem(lax.axis_index("lat"), 2) == turn, north, south)
    out[pl.ds(z.edge_rows - ROWS, ROWS), :] = jnp.zeros((ROWS, LANES), F32)
    for f in range(z.freqs):
        for first in [*range(0, z.half - ROWS, ROWS), z.half - ROWS]:
            eight = flat[pl.ds((f * z.directions + first) * ROWS + start, ROWS, stride=ROWS), :]
            out[pl.ds(f * z.half + first, ROWS), :] = eight


def picks_kernel(z, x, picks):
    lane = lanes()
    for k in range(z.half // 2):
        both = [((lane & (LANES // 2 - 1)) == 2 * k + n).astype(F32) for n in range(2)]
        picks[pl.ds(2 * ROWS * k, 2 * ROWS), :] = jnp.concatenate(both, axis=0).astype(BF16)


def columns_kernel(z, mine, other, picks, local, ecol, wcol, fields, coup, flux, to_east, to_west):
    lane, row = lanes(), rows()
    sec = lax.axis_index("sec")
    total = 2 * z.levels
    for comp in range(2):
        for level in range(z.levels):
            own = level + sec * (z.levels - 1 - 2 * level)
            far = z.levels + level + sec * (z.levels - 1 - 2 * level)
            fields[comp * total + own] = take(mine, comp * z.levels + level)
            fields[comp * total + far] = take(other, comp * z.levels + level)
    sea, diffusion = take(local, 0), take(local, 1)
    top = sec * (total - 1)
    zonal, meridional = fields[top], fields[total + top]
    sums = [take(mine, z.sec_sums + k) + take(other, z.sec_sums + k) for k in range(SUMS)]
    coupling = coupled(sums, zonal, meridional, sea)
    cols = take(mine, z.sec_cols) + take(other, z.sec_cols)
    put(flux, 0, cols)
    for t in range(z.sec_tiles - z.sec_rows):
        put(flux, 1 + t, take(mine, z.sec_rows + t) + take(other, z.sec_rows + t))
    for k in range(4):
        coup[k] = coupling[k]
    arrays = [fields[k] for k in range(z.fields)] + [sea, diffusion] + coupling
    east, west = lane_roll(cols, z.lon_flux), lane_roll(cols, z.lon_flux - SUMS)
    for k, array in enumerate(arrays):
        mine_here = (lane >= HALO * k) & (lane < HALO * (k + 1))
        east = jnp.where(mine_here, lane_roll(array, HALO * (k + 1)), east)
        west = jnp.where(mine_here, lane_roll(array, HALO * k), west)
    for k in range(SUMS):
        edge = jnp.where(row == ROWS - 1, spread(flux, ROWS + k), spread(flux, ROWS + SUMS + k))
        at = z.lon_rows + FLUX_COLS * k
        mine_here = (lane >= at) & (lane < at + FLUX_COLS)
        east = jnp.where(mine_here, lane_roll(edge, at + FLUX_COLS), east)
        west = jnp.where(mine_here, lane_roll(edge, at), west)
    put(to_east, 0, east)
    put(to_west, 0, west)
    for t in range(z.col_tiles):
        put(to_east, 1 + t, take(ecol, t))
        put(to_west, 1 + t, take(wcol, t))


def rows_kernel(z, from_east, from_west, fields, coup, flux, local, got_rows, coup_out, edges, to_first, to_second):
    lane, row = lanes(), rows()
    total = 2 * z.levels
    top = lax.axis_index("sec") * (total - 1)
    sea, diffusion = take(local, 0), take(local, 1)
    cols = take(flux, 0)
    west, east = take(from_west, 0), take(from_east, 0)

    def beyond(first, width):
        near = lane_roll(east, -first)
        far = lane_roll(west, LANES - width - first)
        return jnp.where(lane < width, near, jnp.where(lane >= LANES - width, far, 0.0))

    edge = [beyond(HALO * k, HALO) for k in range(z.fields + 2)]
    for k in range(z.fields + 2):
        edges[k] = edge[k]
    inner, outer = [], []
    for k in range(SUMS):
        at = z.lon_flux + k
        inner.append(jnp.where(lane == 0, lane_roll(west, -at), jnp.where(lane == LANES - 1, lane_roll(east, LANES - 1 - at), 0.0)))
        outer.append(jnp.where(lane == 0, lane_roll(cols, -k), jnp.where(lane == LANES - 1, lane_roll(cols, LANES - 1 - SUMS - k), 0.0)))
    inside = coupled(inner, fields[top], fields[total + top], sea)
    outside = coupled(outer, edges[top], edges[total + top], edge[z.fields])
    main_coupling = [coup[k] + inside[k] for k in range(4)]
    edge_coupling = [beyond(z.lon_coup + HALO * k, HALO) + outside[k] for k in range(4)]
    for k in range(4):
        coup_out[k] = main_coupling[k]
        edges[z.fields + 2 + k] = edge_coupling[k]
    row_edge = [beyond(z.lon_rows + FLUX_COLS * k, FLUX_COLS) for k in range(SUMS)]
    for k in range(SUMS):
        edges[z.arrays + k] = row_edge[k]

    main = [fields[k] for k in range(z.fields)] + [sea, diffusion] + main_coupling
    edge = edge + edge_coupling
    low = row < HALO
    odd = lax.rem(lax.axis_index("lat"), 2) == 1

    def send(index, north, south):
        put(to_first, index, jnp.where(odd, south, north))
        put(to_second, index, jnp.where(odd, north, south))

    def pair(a, b):
        return jnp.where(low, row_roll(b, HALO), a), jnp.where(low, a, row_roll(b, HALO))

    def group(tile, k):
        at = 2 * HALO * k
        in_group = lax.rem(lane + LANES + HALO - at, LANES) < 2 * HALO
        return in_group, lane_roll(tile, at)

    north_edges = jnp.zeros((ROWS, LANES), F32)
    south_edges = north_edges
    for k in range(z.pairs):
        north, south = pair(main[2 * k], main[2 * k + 1])
        send(z.lat_pairs + k, north, south)
        north, south = pair(edge[2 * k], edge[2 * k + 1])
        in_group, moved = group(north, k)
        north_edges = jnp.where(in_group, moved, north_edges)
        in_group, moved = group(south, k)
        south_edges = jnp.where(in_group, moved, south_edges)
    for t in range(z.flux_tiles):
        north, south = jnp.zeros((ROWS, LANES), F32), jnp.zeros((ROWS, LANES), F32)
        north_row, south_row = north, south
        for r in range(min(ROWS, SUMS - t * ROWS)):
            k = t * ROWS + r
            north = jnp.where(row == r, spread(flux, ROWS + k), north)
            south = jnp.where(row == r, spread(flux, ROWS + SUMS + k), south)
            north_row = jnp.where(row == r, jnp.broadcast_to(row_edge[k][ROWS - 1 :], (ROWS, LANES)), north_row)
            south_row = jnp.where(row == r, jnp.broadcast_to(row_edge[k][:1], (ROWS, LANES)), south_row)
        send(z.lat_flux + t, north, south)
        in_group, moved = group(north_row, z.pairs + t)
        north_edges = jnp.where(in_group, moved, north_edges)
        in_group, moved = group(south_row, z.pairs + t)
        south_edges = jnp.where(in_group, moved, south_edges)
    send(z.lat_edges, north_edges, south_edges)


def side_signs(j):
    return (1 if j in (0, 3) else -1), (1 if j in (0, 1) else -1)


def lat_sides(first, second, lat_count):
    place = lax.axis_index("lat")
    odd = lax.rem(place, 2) == 1
    north = jnp.where(place < lat_count - 1, jnp.where(odd, second, first), 0.0)
    south = jnp.where(place > 0, jnp.where(odd, first, second), 0.0)
    return north, south


def wave_kernel(z, lat_count, x, fields, coup, local, coef, picks, from_west, from_east, first, second, out, coup_out, buf, scales, sides, sems):
    q, nf, half = z.quarter, z.freqs, z.half
    lane, row = lanes(), rows()
    total = 2 * z.levels
    top = lax.axis_index("sec") * (total - 1)
    sea = take(local, 0)
    zonal, meridional = current_gain * fields[top], current_gain * fields[total + top]
    coup_out[...] = coup[...]
    place = lax.axis_index("lat")
    odd = lax.rem(place, 2)
    sides[odd] = jnp.where((odd == 1) | (place < lat_count - 1), first[...], 0.0)
    sides[1 - odd] = jnp.where((place > 0) & ((odd == 0) | (place < lat_count - 1)), second[...], 0.0)
    sizes = tables(z.directions)
    headings = []
    for i in range(q):
        c, s = float(sizes[0, i]), float(sizes[1, i])
        for j, heading in enumerate(z.headings(i)):
            sign_x, sign_y = side_signs(j)
            headings.append((heading, i, sign_x, sign_y, 2 * i + (0 if j in (0, 1) else 1)))
            scales[heading] = sea * (1.0 + (sign_x * c) * zonal + (sign_y * s) * meridional)
    ones = jnp.ones((LANES, LANES), BF16)

    def body(f, _):
        speed = spread(coef, f)
        along = [speed * float(sizes[0, i]) for i in range(q)]
        across = [speed * float(sizes[1, i]) for i in range(q)]
        stay = [1.0 - along[i] - across[i] for i in range(q)]
        at = pl.ds(pl.multiple_of((1 + (f // z.per_tile)) * ROWS, ROWS), ROWS)
        back = LANES - half * (f % z.per_tile)
        rims = []
        for ref in (from_west, from_east):
            high, low = parts(lane_roll(ref[at, :], back))
            both = jnp.where(lane < LANES // 2, high, lane_roll(low, LANES // 2))
            both = jnp.concatenate([both, both], axis=0).astype(BF16)
            chosen = jnp.concatenate([both] * (half // 2), axis=0) * picks[...]
            rims.append(jnp.dot(chosen, ones, preferred_element_type=F32))
        for heading, i, sign_x, sign_y, k in headings:
            energy = x[f, heading]
            if sign_x > 0:
                beside = jnp.where(lane == 0, rims[0][k * ROWS : (k + 1) * ROWS], lane_roll(energy, 1))
            else:
                beside = jnp.where(lane == LANES - 1, rims[1][k * ROWS : (k + 1) * ROWS], lane_roll(energy, -1))
            if sign_y > 0:
                below = jnp.where(row == 0, spread(sides.at[1], f * half + heading), row_roll(energy, 1))
            else:
                below = jnp.where(row == ROWS - 1, spread(sides.at[0], f * half + heading - half), row_roll(energy, -1))
            buf[f, heading] = scales[heading] * (stay[i] * energy + along[i] * beside + across[i] * below)
        return 0

    count = 6 if nf % 6 == 0 else 1
    copies = []
    for g in range(count):
        span = pl.ds(g * (nf // count), nf // count)
        lax.fori_loop(g * (nf // count), (g + 1) * (nf // count), body, 0, unroll=3 if nf % 18 == 0 else 1)
        copy = pltpu.make_async_copy(buf.at[span], out.at[span], sems.at[g])
        copy.start()
        copies.append(copy)
    for copy in copies:
        copy.wait()


def ocean_kernel(z, lat_count, from_first, from_second, fields, coup, flux, edges, local, currents_out, ext, force, still, mixed):
    total = 2 * z.levels
    row = rows()
    sec = lax.axis_index("sec")
    sea, diffusion = take(local, 0), take(local, 1)
    low = row < HALO

    def pair(north, south):
        first = jnp.where(low, north, south)
        second = jnp.where(low, row_roll(north, HALO), row_roll(south, HALO))
        return first, second

    def sides(index):
        return lat_sides(take(from_first, index), take(from_second, index), lat_count)

    north_edges, south_edges = sides(z.lat_edges)
    north_rows, south_rows = zip(*[sides(z.lat_flux + t) for t in range(z.flux_tiles)])
    halo, halo_edge = [], []
    for k in range(z.pairs):
        halo += pair(*sides(z.lat_pairs + k))
        halo_edge += [lane_roll(tile, -2 * HALO * k) for tile in pair(north_edges, south_edges)]
    inner, outer, inner_edge, outer_edge = [], [], [], []
    edge_rows = [[lane_roll(tile, -2 * HALO * (z.pairs + t)) for tile in (north_edges, south_edges)] for t in range(z.flux_tiles)]
    for k in range(SUMS):
        t, r = k // ROWS, k % ROWS
        high = row == ROWS - 1
        bottom = row == 0
        north = jnp.broadcast_to(north_rows[t][r : r + 1], (ROWS, LANES))
        south = jnp.broadcast_to(south_rows[t][r : r + 1], (ROWS, LANES))
        inner.append(jnp.where(high, north, jnp.where(bottom, south, 0.0)))
        outer.append(jnp.where(bottom, spread(flux, ROWS + k), jnp.where(high, spread(flux, ROWS + SUMS + k), 0.0)))
        north, south = [jnp.broadcast_to(tile[r : r + 1], (ROWS, LANES)) for tile in edge_rows[t]]
        inner_edge.append(jnp.where(high, north, jnp.where(bottom, south, 0.0)))
        mine = edges[z.arrays + k]
        outer_edge.append(
            jnp.where(bottom, jnp.broadcast_to(mine[ROWS - 1 :], (ROWS, LANES)), jnp.where(high, jnp.broadcast_to(mine[:1], (ROWS, LANES)), 0.0))
        )

    def joined(main, edge, halo_main, halo_side):
        return jnp.concatenate([jnp.concatenate([main, edge], axis=1), jnp.concatenate([halo_main, halo_side], axis=1)], axis=0)

    whole = [joined(fields[k], edges[k], halo[k], halo_edge[k]) for k in range(z.fields)]
    for k in range(z.fields):
        ext[k] = whole[k]
    zonal, meridional = [jnp.where(sec == 0, whole[comp * total], whole[comp * total + total - 1]) for comp in range(2)]
    sea_all = joined(sea, edges[z.fields], halo[z.fields], halo_edge[z.fields])
    kappa = joined(diffusion, edges[z.fields + 1], halo[z.fields + 1], halo_edge[z.fields + 1])
    sums = [joined(inner[k], inner_edge[k], outer[k], outer_edge[k]) for k in range(SUMS)]
    extra = coupled(sums, zonal, meridional, sea_all)
    first = z.fields + 2
    coupling = [joined(coup[k], edges[first + k], halo[first + k], halo_edge[first + k]) + extra[k] for k in range(4)]

    shape = (2 * ROWS, 2 * LANES)
    row_all = lax.broadcasted_iota(jnp.int32, shape, 0)
    row_all = jnp.where(row_all >= 2 * ROWS - HALO, row_all - 2 * ROWS, row_all) + lax.axis_index("lat") * ROWS
    rot = sea_all * (0.05 + 0.1 * (row_all.astype(F32) + 0.5) * (1.0 / (lat_count * ROWS)))
    spin = sea_all * kappa

    def by_level(function, p):
        return jnp.where(sec == 0, function(p), function(total - 1 - p)).astype(F32)

    for p in range(total):
        mix, decay, gain = by_level(lambda level: 0.04 + 0.0125 * (7 * level % 5), p), by_level(lambda level: 1.0 / (1.0 + level), p), by_level(lambda level: stress_gain if level == 0 else 0.0, p)
        force[p] = rot * decay * coupling[1] + sea_all * gain * coupling[2]
        force[total + p] = sea_all * gain * coupling[3] - rot * decay * coupling[0]
        mixed[p] = sea_all * mix
        still[p] = sea_all * (1.0 - mix * (1 if p in (0, total - 1) else 2)) - 4.0 * spin
    for step in range(ITERS):
        needed = min(total, z.levels + ITERS - 1 - step)
        every = [ext[comp * total + p] for comp in range(2) for p in range(needed)]
        after = []
        for comp in range(2):
            for p in range(needed):
                at = comp * needed + p
                value = every[at]
                around = (pltpu.roll(value, 1, 1) + pltpu.roll(value, 2 * LANES - 1, 1)) + (pltpu.roll(value, 1, 0) + pltpu.roll(value, 2 * ROWS - 1, 0))
                near = [ext[comp * total + other] for other in (p - 1, p + 1) if 0 <= other < total]
                turned = rot * ext[(1 - comp) * total + p]
                moved = still[p] * value + spin * around + mixed[p] * sum(near[1:], near[0]) + force[comp * total + p]
                after.append(moved + turned if comp == 0 else moved - turned)
        if step < ITERS - 1:
            for comp in range(2):
                for p in range(needed):
                    ext[comp * total + p] = after[comp * needed + p]
        else:
            for comp in range(2):
                for level in range(z.levels):
                    place = level + sec * (z.levels - 1 - 2 * level)
                    currents_out[comp, place] = after[comp * needed + level][:ROWS, :LANES]


def tables(directions):
    quarter = directions // 4
    heading = (np.arange(quarter) + 0.5) * (2.0 * math.pi / directions)
    return np.stack([np.cos(heading), np.sin(heading)]).astype(np.float32)


def shifted(value, axis, steps):
    count = lax.axis_size(axis)
    return lax.ppermute(value, axis, [(i, (i + steps) % count) for i in range(count)])


def swapped(value, parity):
    lat, lon = lax.axis_size("lat"), lax.axis_size("lon")
    pairs = []
    for i in range(lat):
        other = i + 1 if i % 2 == parity else i - 1
        for j in range(lon):
            if 0 <= other < lat:
                pairs.append((i * lon + j, other * lon + j))
            elif j ^ 1 < lon:
                pairs.append((i * lon + j, i * lon + (j ^ 1)))
    return lax.ppermute(value, ("lat", "lon"), pairs)


def flat(tiles):
    return jax.ShapeDtypeStruct((tiles * ROWS, LANES), F32)


def stack(count):
    return jax.ShapeDtypeStruct((count, ROWS, LANES), F32)


def call(kernel, out_shape, in_specs, out_specs=None, scratch=(), name=None, bytes_accessed=0, flops=0):
    return pl.pallas_call(
        kernel,
        out_shape=out_shape,
        in_specs=in_specs,
        out_specs=out_specs if out_specs is not None else [VMEM] * len(out_shape),
        scratch_shapes=list(scratch),
        name=name,
        compiler_params=pltpu.CompilerParams(vmem_limit_bytes=24 * 1024 * 1024),
        cost_estimate=pl.CostEstimate(flops=flops, bytes_accessed=bytes_accessed, transcendentals=0),
    )


def shards(spectra, currents, land_mask, diffusion, courant, stokes_weight, stress_weight):
    freqs, directions, tile_rows, tile_cols = spectra.shape
    levels = currents.shape[1]
    lat_count = lax.axis_size("lat")
    assert lax.axis_size("sec") == 2 and (tile_rows, tile_cols) == (ROWS, LANES) and directions % 4 == 0
    z = Sizes(freqs, directions, levels)
    size = spectra.size * 4
    copies = 4 * len(chunks(z))
    sems = pltpu.SemaphoreType.DMA((copies,))
    whole = pltpu.VMEM(spectra.shape, F32)

    edge_rows = jax.ShapeDtypeStruct((z.edge_rows, LANES), F32)
    inputs = (spectra, currents, land_mask, diffusion, courant, stokes_weight, stress_weight)
    kept, pay, ecol, wcol, local, coef = call(
        functools.partial(sums_kernel, z),
        (
            whole,
            flat(z.sec_tiles),
            flat(z.col_tiles),
            flat(z.col_tiles),
            flat(2),
            flat(z.coef_tiles),
        ),
        [ANY] * 7,
        scratch=[
            pltpu.VMEM(currents.shape, F32),
            pltpu.VMEM(land_mask.shape, jnp.int32),
            pltpu.SMEM(courant.shape, F32),
            pltpu.SMEM(courant.shape, F32),
            pltpu.SMEM(courant.shape, F32),
            pltpu.VMEM((5 * SUMS, ROWS, LANES), F32),
            sems,
            pltpu.SemaphoreType.DMA((6,)),
        ],
        name="spectra_sums",
        bytes_accessed=size,
        flops=16 * size // 4,
    )(*[pltpu.with_memory_space_constraint(array, pltpu.HBM) for array in inputs])

    other = shifted(pay, "sec", 1)

    got_first, got_second = [
        swapped(
            call(
                functools.partial(edge_rows_kernel, z, turn),
                (edge_rows,),
                [VMEM],
                name="pick_rows",
                bytes_accessed=size // 16,
                flops=2**16,
            )(kept)[0],
            turn,
        )
        for turn in range(2)
    ]

    (picks,) = call(
        functools.partial(picks_kernel, z),
        (jax.ShapeDtypeStruct((z.half * ROWS, LANES), BF16),),
        [VMEM],
        name="picks",
        bytes_accessed=size,
        flops=8388608,
    )(kept)

    fields, coup, flux, to_east, to_west = call(
        functools.partial(columns_kernel, z),
        (stack(z.fields), stack(4), flat(1 + z.sec_tiles - z.sec_rows), flat(1 + z.col_tiles), flat(1 + z.col_tiles)),
        [VMEM] * 6,
        name="pack_columns",
        bytes_accessed=2**18,
        flops=1073741824,
    )(pay, other, picks, local, ecol, wcol)

    from_east = shifted(to_west, "lon", -1)
    from_west = shifted(to_east, "lon", 1)

    coup, edges, to_first, to_second = call(
        functools.partial(rows_kernel, z),
        (stack(4), stack(z.arrays + SUMS), flat(z.lat_tiles), flat(z.lat_tiles)),
        [VMEM] * 7,
        name="pack_rows",
        bytes_accessed=2**18,
        flops=2**27,
    )(from_east, from_west, fields, coup, flux, local, got_second)

    from_second = swapped(to_second, 1)
    from_first = swapped(to_first, 0)

    new_spectra, coup = call(
        functools.partial(wave_kernel, z, lat_count),
        (jax.ShapeDtypeStruct(spectra.shape, F32), stack(4)),
        [VMEM] * 10,
        out_specs=[ANY, VMEM],
        scratch=[whole, pltpu.VMEM((directions, ROWS, LANES), F32), pltpu.VMEM((2, z.edge_rows, LANES), F32), sems],
        name="wave_step",
        bytes_accessed=2 * size,
        flops=9 * size // 4,
    )(kept, fields, coup, local, coef, picks, from_west, from_east, got_first, got_second)

    (new_currents,) = call(
        functools.partial(ocean_kernel, z, lat_count),
        (jax.ShapeDtypeStruct(currents.shape, F32),),
        [VMEM] * 7,
        scratch=[pltpu.VMEM((count, 2 * ROWS, 2 * LANES), F32) for count in (z.fields, z.fields, 2 * levels, 2 * levels)],
        name="ocean_steps",
        bytes_accessed=2**20,
        flops=2**20,
    )(from_first, from_second, fields, coup, flux, edges, local)
    return new_spectra, new_currents


def solution(mesh):
    in_specs = (
        P("sec", None, "lat", "lon"),
        P(None, "sec", "lat", "lon"),
        P("lat", "lon"),
        P("lat", "lon"),
        P("sec"),
        P("sec"),
        P("sec"),
    )
    out_specs = (P("sec", None, "lat", "lon"), P(None, "sec", "lat", "lon"))
    return jax.shard_map(shards, mesh=mesh, in_specs=in_specs, out_specs=out_specs, check_vma=False)
```

```python
import functools
import math

import jax
import jax.numpy as jnp
import numpy as np
from jax import lax
from jax.experimental import pallas as pl
from jax.experimental.pallas import tpu as pltpu
from jax.sharding import PartitionSpec as P

ITERS = 4
ROWS = 8
LANES = 128
HALO = 4
MOMENTS = 5
SUMS = 2 * MOMENTS
FLUX_COLS = 3
current_gain = 0.1
stress_gain = 0.5

VMEM = pl.BlockSpec(memory_space=pltpu.VMEM)
SMEM = pl.BlockSpec(memory_space=pltpu.SMEM)
ANY = pl.BlockSpec(memory_space=pl.ANY)
F32 = jnp.float32
BF16 = jnp.bfloat16


def lanes():
    return lax.broadcasted_iota(jnp.int32, (ROWS, LANES), 1)


def rows():
    return lax.broadcasted_iota(jnp.int32, (ROWS, LANES), 0)


def lane_roll(tile, shift):
    if isinstance(shift, int):
        shift %= LANES
        if shift == 0:
            return tile
    return pltpu.roll(tile, shift, 1)


def row_roll(tile, shift):
    shift %= ROWS
    return tile if shift == 0 else pltpu.roll(tile, shift, 0)


def spread(ref, row):
    return jnp.broadcast_to(ref[pl.ds(row, 1), :], (ROWS, LANES))


def put(ref, index, tile):
    ref[pl.ds(index * ROWS, ROWS), :] = tile


def take(ref, index):
    return ref[pl.ds(index * ROWS, ROWS), :]


def coupled(sums, zonal, meridional, sea):
    result = []
    for w in range(2):
        c, s, cc, cs, ss = sums[w * MOMENTS : (w + 1) * MOMENTS]
        result.append(sea * (c + current_gain * (zonal * cc + meridional * cs)))
        result.append(sea * (s + current_gain * (zonal * cs + meridional * ss)))
    return result


class Sizes:
    def __init__(self, freqs, directions, levels):
        self.freqs = freqs
        self.directions = directions
        self.levels = levels
        self.quarter = directions // 4
        self.fields = 2 * 2 * levels
        self.half = directions // 2
        self.per_tile = LANES // self.half
        self.col_tiles = -(-freqs // self.per_tile)
        self.edge_rows = -(-freqs * directions // 2 // ROWS) * ROWS
        assert self.half >= ROWS
        self.sec_sums = self.fields // 2
        self.sec_cols = self.sec_sums + SUMS
        self.sec_rows = self.sec_cols + 1
        self.sec_tiles = self.sec_rows + -(-2 * SUMS // ROWS)
        self.lon_coup = HALO * (self.fields + 2)
        self.lon_flux = self.lon_coup + 4 * HALO
        self.lon_rows = self.lon_flux + SUMS
        self.arrays = self.fields + 2 + 4
        total = 2 * levels
        assert ITERS <= HALO and HALO + levels - 1 - (total - 2) <= 2
        self.short = [comp * total + p for comp in range(2) for p in range(total - 2, total)]
        self.long = [k for k in range(self.arrays) if k not in self.short]
        self.pairs = len(self.long) // 2
        self.bodies = self.pairs + 1
        self.flux_tiles = -(-SUMS // ROWS)
        self.lat_pairs = 0
        self.lat_flux = self.lat_pairs + self.bodies
        self.lat_edges = self.lat_flux + self.flux_tiles
        self.lat_tiles = self.lat_edges + 1
        self.coef_tiles = -(-freqs // ROWS)
        assert self.lon_rows + SUMS * FLUX_COLS <= LANES
        assert (self.bodies + self.flux_tiles) * 2 * HALO <= LANES

    def headings(self, i):
        q = self.quarter
        return (i, 2 * q - 1 - i, 2 * q + i, 4 * q - 1 - i)


def chunks(z):
    q = z.quarter
    cuts = sorted({0, q * 5 // 9, q})
    result = []
    for lo, hi in zip(cuts, cuts[1:]):
        starts = (lo, 2 * q - hi, 2 * q + lo, 4 * q - hi)
        result.append((lo, hi, [pl.ds(start, hi - lo) for start in starts]))
    return result


def sums_kernel(z, x, cur_in, mask_in, diffusion_in, courant_in, stokes_in, stress_in, buf, pay, ecol, wcol, local, coef, cur, mask, courant, stokes, stress, acc, sems, small_sems):
    q, nf = z.quarter, z.freqs
    pairs = ((cur_in, cur), (mask_in, mask), (diffusion_in, local.at[pl.ds(ROWS, ROWS)]), (courant_in, courant), (stokes_in, stokes), (stress_in, stress))
    small = [pltpu.make_async_copy(source, target, small_sems.at[k]) for k, (source, target) in enumerate(pairs)]
    for copy in small:
        copy.start()
    copies = []
    for g, (_, _, spans) in enumerate(chunks(z)):
        for j, span in enumerate(spans):
            copies.append(pltpu.make_async_copy(x.at[:, span], buf.at[:, span], sems.at[4 * g + j]))
    for copy in copies:
        copy.start()

    lane, row = lanes(), rows()
    zero = jnp.zeros((ROWS, LANES), F32)
    for k in range(5 * SUMS):
        acc[k] = zero
    sizes = tables(z.directions)
    east, west = [zero] * z.col_tiles, [zero] * z.col_tiles
    for copy in small:
        copy.wait()
    sea = mask[...].astype(F32)
    put(local, 0, sea)
    for comp in range(2):
        for level in range(z.levels):
            put(pay, comp * z.levels + level, cur[comp, level] * sea)
    for t in range(z.coef_tiles):
        tile = zero
        for f in range(t * ROWS, min(nf, (t + 1) * ROWS)):
            tile = jnp.where(row == f - t * ROWS, courant[f], tile)
        put(coef, t, tile)

    def add(i):
        c, s = float(sizes[0, i]), float(sizes[1, i])
        heading = z.headings(i)
        total = [[zero] * 4 for _ in range(4)]
        for f in range(nf):
            t = f // z.per_tile
            cg = courant[f]
            factors = (stokes[f], stokes[f] * cg, stress[f], stress[f] * cg)
            for j in range(4):
                energy = buf[f, heading[j]]
                for k in range(4):
                    total[k][j] = total[k][j] + factors[k] * energy
                at = f % z.per_tile * z.half + 2 * i + (0 if j in (0, 1) else 1)
                if j in (0, 3):
                    east[t] = jnp.where(lane == at, lane_roll(energy, at - (LANES - 1)), east[t])
                else:
                    west[t] = jnp.where(lane == at, lane_roll(energy, at), west[t])
        cc, cs, ss = c * c, c * s, s * s
        for w in range(2):
            plain, fast = total[2 * w], total[2 * w + 1]
            both = c + s
            h = [plain[j] - both * fast[j] for j in range(4)]
            here, there = h[0] + h[3], h[1] + h[2]
            every = here + there
            values = [
                c * (here - there),
                s * ((h[0] + h[1]) - (h[2] + h[3])),
                cc * every,
                cs * ((h[0] - h[3]) + (h[2] - h[1])),
                ss * every,
            ]
            for a, b, size, signs in (
                (fast[0] + fast[3], fast[0] - fast[3], c, (1, 1, 1)),
                (fast[1] + fast[2], fast[1] - fast[2], c, (-1, 1, -1)),
            ):
                values += [signs[0] * size * c * a, signs[1] * size * s * b, size * cc * a, signs[2] * size * cs * b, size * ss * a]
            for a, b, size, signs in (
                (fast[0] + fast[1], fast[0] - fast[1], s, (1, 1, 1)),
                (fast[2] + fast[3], fast[3] - fast[2], s, (1, -1, -1)),
            ):
                values += [signs[0] * size * c * b, signs[1] * size * s * a, size * cc * a, signs[2] * size * cs * b, size * ss * a]
            for kind in range(5):
                for m in range(MOMENTS):
                    at = kind * SUMS + w * MOMENTS + m
                    acc[at] = acc[at] + values[kind * MOMENTS + m]

    for g, (lo, hi, _) in enumerate(chunks(z)):
        for copy in copies[4 * g : 4 * g + 4]:
            copy.wait()
        for i in range(lo, hi):
            add(i)
    for t in range(z.col_tiles):
        put(ecol, t, east[t])
        put(wcol, t, west[t])

    cols = zero
    rims = [zero] * (z.sec_tiles - z.sec_rows)
    for k in range(SUMS):
        center, east, west, north, south = (acc[kind * SUMS + k] for kind in range(5))
        value = center + jnp.where(lane > 0, lane_roll(east, 1), 0.0) + jnp.where(lane < LANES - 1, lane_roll(west, -1), 0.0)
        value = value + jnp.where(row > 0, row_roll(north, 1), 0.0) + jnp.where(row < ROWS - 1, row_roll(south, -1), 0.0)
        put(pay, z.sec_sums + k, value)
        cols = jnp.where(lane == k, lane_roll(east, k - (LANES - 1)), cols)
        cols = jnp.where(lane == SUMS + k, lane_roll(west, SUMS + k), cols)
        for at, tile, edge in ((k, north, ROWS - 1), (SUMS + k, south, 0)):
            t, r = at // ROWS, at % ROWS
            rims[t] = jnp.where(row == r, row_roll(tile, r - edge), rims[t])
    put(pay, z.sec_cols, cols)
    for t, tile in enumerate(rims):
        put(pay, z.sec_rows + t, tile)


def parts(tile):
    high = tile.astype(BF16).astype(F32)
    return high, (tile - high).astype(BF16).astype(F32)


def edge_rows_kernel(z, turn, x, out):
    flat = x.reshape(z.freqs * z.directions * ROWS, LANES)
    north, south = ROWS - 1, z.half * ROWS
    start = jnp.where(lax.rem(lax.axis_index("lat"), 2) == turn, north, south)
    out[pl.ds(z.edge_rows - ROWS, ROWS), :] = jnp.zeros((ROWS, LANES), F32)
    for f in range(z.freqs):
        for first in [*range(0, z.half - ROWS, ROWS), z.half - ROWS]:
            eight = flat[pl.ds((f * z.directions + first) * ROWS + start, ROWS, stride=ROWS), :]
            out[pl.ds(f * z.half + first, ROWS), :] = eight


def picks_kernel(z, x, picks):
    lane = lanes()
    for k in range(z.half // 2):
        both = [((lane & (LANES // 2 - 1)) == 2 * k + n).astype(F32) for n in range(2)]
        picks[pl.ds(2 * ROWS * k, 2 * ROWS), :] = jnp.concatenate(both, axis=0).astype(BF16)


def columns_kernel(z, mine, other, picks, local, ecol, wcol, fields, coup, flux, to_east, to_west):
    lane, row = lanes(), rows()
    sec = lax.axis_index("sec")
    total = 2 * z.levels
    for comp in range(2):
        for level in range(z.levels):
            own = level + sec * (z.levels - 1 - 2 * level)
            far = z.levels + level + sec * (z.levels - 1 - 2 * level)
            fields[comp * total + own] = take(mine, comp * z.levels + level)
            fields[comp * total + far] = take(other, comp * z.levels + level)
    sea, diffusion = take(local, 0), take(local, 1)
    top = sec * (total - 1)
    zonal, meridional = fields[top], fields[total + top]
    sums = [take(mine, z.sec_sums + k) + take(other, z.sec_sums + k) for k in range(SUMS)]
    coupling = coupled(sums, zonal, meridional, sea)
    cols = take(mine, z.sec_cols) + take(other, z.sec_cols)
    put(flux, 0, cols)
    for t in range(z.sec_tiles - z.sec_rows):
        put(flux, 1 + t, take(mine, z.sec_rows + t) + take(other, z.sec_rows + t))
    for k in range(4):
        coup[k] = coupling[k]
    arrays = [fields[k] for k in range(z.fields)] + [sea, diffusion] + coupling
    east, west = lane_roll(cols, z.lon_flux), lane_roll(cols, z.lon_flux - SUMS)
    for k, array in enumerate(arrays):
        mine_here = (lane >= HALO * k) & (lane < HALO * (k + 1))
        east = jnp.where(mine_here, lane_roll(array, HALO * (k + 1)), east)
        west = jnp.where(mine_here, lane_roll(array, HALO * k), west)
    for k in range(SUMS):
        edge = jnp.where(row == ROWS - 1, spread(flux, ROWS + k), spread(flux, ROWS + SUMS + k))
        at = z.lon_rows + FLUX_COLS * k
        mine_here = (lane >= at) & (lane < at + FLUX_COLS)
        east = jnp.where(mine_here, lane_roll(edge, at + FLUX_COLS), east)
        west = jnp.where(mine_here, lane_roll(edge, at), west)
    put(to_east, 0, east)
    put(to_west, 0, west)
    for t in range(z.col_tiles):
        put(to_east, 1 + t, take(ecol, t))
        put(to_west, 1 + t, take(wcol, t))


def rows_kernel(z, from_east, from_west, fields, coup, flux, local, got_rows, coup_out, edges, to_first, to_second):
    lane, row = lanes(), rows()
    total = 2 * z.levels
    top = lax.axis_index("sec") * (total - 1)
    sea, diffusion = take(local, 0), take(local, 1)
    cols = take(flux, 0)
    west, east = take(from_west, 0), take(from_east, 0)

    def beyond(first, width):
        near = lane_roll(east, -first)
        far = lane_roll(west, LANES - width - first)
        return jnp.where(lane < width, near, jnp.where(lane >= LANES - width, far, 0.0))

    edge = [beyond(HALO * k, HALO) for k in range(z.fields + 2)]
    for k in range(z.fields + 2):
        edges[k] = edge[k]
    inner, outer = [], []
    for k in range(SUMS):
        at = z.lon_flux + k
        inner.append(jnp.where(lane == 0, lane_roll(west, -at), jnp.where(lane == LANES - 1, lane_roll(east, LANES - 1 - at), 0.0)))
        outer.append(jnp.where(lane == 0, lane_roll(cols, -k), jnp.where(lane == LANES - 1, lane_roll(cols, LANES - 1 - SUMS - k), 0.0)))
    inside = coupled(inner, fields[top], fields[total + top], sea)
    outside = coupled(outer, edges[top], edges[total + top], edge[z.fields])
    main_coupling = [coup[k] + inside[k] for k in range(4)]
    edge_coupling = [beyond(z.lon_coup + HALO * k, HALO) + outside[k] for k in range(4)]
    for k in range(4):
        coup_out[k] = main_coupling[k]
        edges[z.fields + 2 + k] = edge_coupling[k]
    row_edge = [beyond(z.lon_rows + FLUX_COLS * k, FLUX_COLS) for k in range(SUMS)]
    for k in range(SUMS):
        edges[z.arrays + k] = row_edge[k]

    main = [fields[k] for k in range(z.fields)] + [sea, diffusion] + main_coupling
    edge = edge + edge_coupling
    low = row < HALO
    odd = lax.rem(lax.axis_index("lat"), 2) == 1

    def send(index, north, south):
        put(to_first, index, jnp.where(odd, south, north))
        put(to_second, index, jnp.where(odd, north, south))

    def pair(a, b):
        return jnp.where(low, row_roll(b, HALO), a), jnp.where(low, a, row_roll(b, HALO))

    def group(tile, k):
        at = 2 * HALO * k
        in_group = lax.rem(lane + LANES + HALO - at, LANES) < 2 * HALO
        return in_group, lane_roll(tile, at)

    north_edges = jnp.zeros((ROWS, LANES), F32)
    south_edges = north_edges
    def four(tiles):
        north, south = tiles[0], tiles[0]
        for j in range(1, 4):
            north = jnp.where(lax.div(row, 2) == 3 - j, row_roll(tiles[j], -2 * j), north)
            south = jnp.where(lax.div(row, 2) == j, row_roll(tiles[j], 2 * j), south)
        return north, south

    for k in range(z.bodies):
        both = []
        for arrays in (main, edge):
            if k < z.pairs:
                both.append(pair(*[arrays[n] for n in z.long[2 * k : 2 * k + 2]]))
            else:
                both.append(four([arrays[n] for n in z.short]))
        send(z.lat_pairs + k, *both[0])
        north, south = both[1]
        in_group, moved = group(north, k)
        north_edges = jnp.where(in_group, moved, north_edges)
        in_group, moved = group(south, k)
        south_edges = jnp.where(in_group, moved, south_edges)
    for t in range(z.flux_tiles):
        north, south = jnp.zeros((ROWS, LANES), F32), jnp.zeros((ROWS, LANES), F32)
        north_row, south_row = north, south
        for r in range(min(ROWS, SUMS - t * ROWS)):
            k = t * ROWS + r
            north = jnp.where(row == r, spread(flux, ROWS + k), north)
            south = jnp.where(row == r, spread(flux, ROWS + SUMS + k), south)
            north_row = jnp.where(row == r, jnp.broadcast_to(row_edge[k][ROWS - 1 :], (ROWS, LANES)), north_row)
            south_row = jnp.where(row == r, jnp.broadcast_to(row_edge[k][:1], (ROWS, LANES)), south_row)
        send(z.lat_flux + t, north, south)
        in_group, moved = group(north_row, z.bodies + t)
        north_edges = jnp.where(in_group, moved, north_edges)
        in_group, moved = group(south_row, z.bodies + t)
        south_edges = jnp.where(in_group, moved, south_edges)
    send(z.lat_edges, north_edges, south_edges)


def side_signs(j):
    return (1 if j in (0, 3) else -1), (1 if j in (0, 1) else -1)


def lat_sides(first, second, lat_count):
    place = lax.axis_index("lat")
    odd = lax.rem(place, 2) == 1
    north = jnp.where(place < lat_count - 1, jnp.where(odd, second, first), 0.0)
    south = jnp.where(place > 0, jnp.where(odd, first, second), 0.0)
    return north, south


def wave_kernel(z, lat_count, x, fields, coup, local, coef, picks, from_west, from_east, first, second, out, coup_out, buf, scales, sides, sems):
    q, nf, half = z.quarter, z.freqs, z.half
    lane, row = lanes(), rows()
    total = 2 * z.levels
    top = lax.axis_index("sec") * (total - 1)
    sea = take(local, 0)
    zonal, meridional = current_gain * fields[top], current_gain * fields[total + top]
    coup_out[...] = coup[...]
    place = lax.axis_index("lat")
    odd = lax.rem(place, 2)
    sides[odd] = jnp.where((odd == 1) | (place < lat_count - 1), first[...], 0.0)
    sides[1 - odd] = jnp.where((place > 0) & ((odd == 0) | (place < lat_count - 1)), second[...], 0.0)
    sizes = tables(z.directions)
    headings = []
    for i in range(q):
        c, s = float(sizes[0, i]), float(sizes[1, i])
        for j, heading in enumerate(z.headings(i)):
            sign_x, sign_y = side_signs(j)
            headings.append((heading, i, sign_x, sign_y, 2 * i + (0 if j in (0, 1) else 1)))
            scales[heading] = sea * (1.0 + (sign_x * c) * zonal + (sign_y * s) * meridional)
    ones = jnp.ones((LANES, LANES), BF16)

    def body(f, _):
        speed = spread(coef, f)
        along = [speed * float(sizes[0, i]) for i in range(q)]
        across = [speed * float(sizes[1, i]) for i in range(q)]
        stay = [1.0 - along[i] - across[i] for i in range(q)]
        at = pl.ds(pl.multiple_of((1 + (f // z.per_tile)) * ROWS, ROWS), ROWS)
        back = LANES - half * (f % z.per_tile)
        rims = []
        for ref in (from_west, from_east):
            high, low = parts(lane_roll(ref[at, :], back))
            both = jnp.where(lane < LANES // 2, high, lane_roll(low, LANES // 2))
            both = jnp.concatenate([both, both], axis=0).astype(BF16)
            chosen = jnp.concatenate([both] * (half // 2), axis=0) * picks[...]
            rims.append(jnp.dot(chosen, ones, preferred_element_type=F32))
        for heading, i, sign_x, sign_y, k in headings:
            energy = x[f, heading]
            if sign_x > 0:
                beside = jnp.where(lane == 0, rims[0][k * ROWS : (k + 1) * ROWS], lane_roll(energy, 1))
            else:
                beside = jnp.where(lane == LANES - 1, rims[1][k * ROWS : (k + 1) * ROWS], lane_roll(energy, -1))
            if sign_y > 0:
                below = jnp.where(row == 0, spread(sides.at[1], f * half + heading), row_roll(energy, 1))
            else:
                below = jnp.where(row == ROWS - 1, spread(sides.at[0], f * half + heading - half), row_roll(energy, -1))
            buf[f, heading] = scales[heading] * (stay[i] * energy + along[i] * beside + across[i] * below)
        return 0

    count = 6 if nf % 6 == 0 else 1
    copies = []
    for g in range(count):
        span = pl.ds(g * (nf // count), nf // count)
        lax.fori_loop(g * (nf // count), (g + 1) * (nf // count), body, 0, unroll=3 if nf % 18 == 0 else 1)
        copy = pltpu.make_async_copy(buf.at[span], out.at[span], sems.at[g])
        copy.start()
        copies.append(copy)
    for copy in copies:
        copy.wait()


def ocean_kernel(z, lat_count, from_first, from_second, fields, coup, flux, edges, local, currents_out, ext, force, still, mixed):
    total = 2 * z.levels
    row = rows()
    sec = lax.axis_index("sec")
    sea, diffusion = take(local, 0), take(local, 1)
    low = row < HALO

    def pair(north, south):
        first = jnp.where(low, north, south)
        second = jnp.where(low, row_roll(north, HALO), row_roll(south, HALO))
        return first, second

    def sides(index):
        return lat_sides(take(from_first, index), take(from_second, index), lat_count)

    north_edges, south_edges = sides(z.lat_edges)
    north_rows, south_rows = zip(*[sides(z.lat_flux + t) for t in range(z.flux_tiles)])
    def four(north, south):
        return [jnp.where(row < 2, row_roll(north, -2 * j), jnp.where(row >= ROWS - 2, row_roll(south, 2 * j), 0.0)) for j in range(4)]

    halo, halo_edge = {}, {}
    for k in range(z.bodies):
        places, split = (z.long[2 * k : 2 * k + 2], pair) if k < z.pairs else (z.short, four)
        halo.update(zip(places, split(*sides(z.lat_pairs + k))))
        halo_edge.update(zip(places, [lane_roll(tile, -2 * HALO * k) for tile in split(north_edges, south_edges)]))
    inner, outer, inner_edge, outer_edge = [], [], [], []
    edge_rows = [[lane_roll(tile, -2 * HALO * (z.bodies + t)) for tile in (north_edges, south_edges)] for t in range(z.flux_tiles)]
    for k in range(SUMS):
        t, r = k // ROWS, k % ROWS
        high = row == ROWS - 1
        bottom = row == 0
        north = jnp.broadcast_to(north_rows[t][r : r + 1], (ROWS, LANES))
        south = jnp.broadcast_to(south_rows[t][r : r + 1], (ROWS, LANES))
        inner.append(jnp.where(high, north, jnp.where(bottom, south, 0.0)))
        outer.append(jnp.where(bottom, spread(flux, ROWS + k), jnp.where(high, spread(flux, ROWS + SUMS + k), 0.0)))
        north, south = [jnp.broadcast_to(tile[r : r + 1], (ROWS, LANES)) for tile in edge_rows[t]]
        inner_edge.append(jnp.where(high, north, jnp.where(bottom, south, 0.0)))
        mine = edges[z.arrays + k]
        outer_edge.append(
            jnp.where(bottom, jnp.broadcast_to(mine[ROWS - 1 :], (ROWS, LANES)), jnp.where(high, jnp.broadcast_to(mine[:1], (ROWS, LANES)), 0.0))
        )

    def joined(main, edge, halo_main, halo_side):
        return jnp.concatenate([jnp.concatenate([main, edge], axis=1), jnp.concatenate([halo_main, halo_side], axis=1)], axis=0)

    whole = [joined(fields[k], edges[k], halo[k], halo_edge[k]) for k in range(z.fields)]
    for k in range(z.fields):
        ext[k] = whole[k]
    zonal, meridional = [jnp.where(sec == 0, whole[comp * total], whole[comp * total + total - 1]) for comp in range(2)]
    sea_all = joined(sea, edges[z.fields], halo[z.fields], halo_edge[z.fields])
    kappa = joined(diffusion, edges[z.fields + 1], halo[z.fields + 1], halo_edge[z.fields + 1])
    sums = [joined(inner[k], inner_edge[k], outer[k], outer_edge[k]) for k in range(SUMS)]
    extra = coupled(sums, zonal, meridional, sea_all)
    first = z.fields + 2
    coupling = [joined(coup[k], edges[first + k], halo[first + k], halo_edge[first + k]) + extra[k] for k in range(4)]

    shape = (2 * ROWS, 2 * LANES)
    row_all = lax.broadcasted_iota(jnp.int32, shape, 0)
    row_all = jnp.where(row_all >= 2 * ROWS - HALO, row_all - 2 * ROWS, row_all) + lax.axis_index("lat") * ROWS
    rot = sea_all * (0.05 + 0.1 * (row_all.astype(F32) + 0.5) * (1.0 / (lat_count * ROWS)))
    spin = sea_all * kappa

    def by_level(function, p):
        return jnp.where(sec == 0, function(p), function(total - 1 - p)).astype(F32)

    for p in range(total):
        mix, decay, gain = by_level(lambda level: 0.04 + 0.0125 * (7 * level % 5), p), by_level(lambda level: 1.0 / (1.0 + level), p), by_level(lambda level: stress_gain if level == 0 else 0.0, p)
        force[p] = rot * decay * coupling[1] + sea_all * gain * coupling[2]
        force[total + p] = sea_all * gain * coupling[3] - rot * decay * coupling[0]
        mixed[p] = sea_all * mix
        still[p] = sea_all * (1.0 - mix * (1 if p in (0, total - 1) else 2)) - 4.0 * spin
    for step in range(ITERS):
        needed = min(total, z.levels + ITERS - 1 - step)
        every = [ext[comp * total + p] for comp in range(2) for p in range(needed)]
        after = []
        for comp in range(2):
            for p in range(needed):
                at = comp * needed + p
                value = every[at]
                around = (pltpu.roll(value, 1, 1) + pltpu.roll(value, 2 * LANES - 1, 1)) + (pltpu.roll(value, 1, 0) + pltpu.roll(value, 2 * ROWS - 1, 0))
                near = [ext[comp * total + other] for other in (p - 1, p + 1) if 0 <= other < total]
                turned = rot * ext[(1 - comp) * total + p]
                moved = still[p] * value + spin * around + mixed[p] * sum(near[1:], near[0]) + force[comp * total + p]
                after.append(moved + turned if comp == 0 else moved - turned)
        if step < ITERS - 1:
            for comp in range(2):
                for p in range(needed):
                    ext[comp * total + p] = after[comp * needed + p]
        else:
            for comp in range(2):
                for level in range(z.levels):
                    place = level + sec * (z.levels - 1 - 2 * level)
                    currents_out[comp, place] = after[comp * needed + level][:ROWS, :LANES]


def tables(directions):
    quarter = directions // 4
    heading = (np.arange(quarter) + 0.5) * (2.0 * math.pi / directions)
    return np.stack([np.cos(heading), np.sin(heading)]).astype(np.float32)


def shifted(value, axis, steps):
    count = lax.axis_size(axis)
    return lax.ppermute(value, axis, [(i, (i + steps) % count) for i in range(count)])


def swapped(value, parity):
    lat, lon = lax.axis_size("lat"), lax.axis_size("lon")
    pairs = []
    for i in range(lat):
        other = i + 1 if i % 2 == parity else i - 1
        for j in range(lon):
            if 0 <= other < lat:
                pairs.append((i * lon + j, other * lon + j))
            elif j ^ 1 < lon:
                pairs.append((i * lon + j, i * lon + (j ^ 1)))
    return lax.ppermute(value, ("lat", "lon"), pairs)


def flat(tiles):
    return jax.ShapeDtypeStruct((tiles * ROWS, LANES), F32)


def stack(count):
    return jax.ShapeDtypeStruct((count, ROWS, LANES), F32)


def call(kernel, out_shape, in_specs, out_specs=None, scratch=(), name=None, bytes_accessed=0, flops=0):
    return pl.pallas_call(
        kernel,
        out_shape=out_shape,
        in_specs=in_specs,
        out_specs=out_specs if out_specs is not None else [VMEM] * len(out_shape),
        scratch_shapes=list(scratch),
        name=name,
        compiler_params=pltpu.CompilerParams(vmem_limit_bytes=24 * 1024 * 1024),
        cost_estimate=pl.CostEstimate(flops=flops, bytes_accessed=bytes_accessed, transcendentals=0),
    )


def shards(spectra, currents, land_mask, diffusion, courant, stokes_weight, stress_weight):
    freqs, directions, tile_rows, tile_cols = spectra.shape
    levels = currents.shape[1]
    lat_count = lax.axis_size("lat")
    assert lax.axis_size("sec") == 2 and (tile_rows, tile_cols) == (ROWS, LANES) and directions % 4 == 0
    z = Sizes(freqs, directions, levels)
    size = spectra.size * 4
    copies = 4 * len(chunks(z))
    sems = pltpu.SemaphoreType.DMA((copies,))
    whole = pltpu.VMEM(spectra.shape, F32)

    edge_rows = jax.ShapeDtypeStruct((z.edge_rows, LANES), F32)
    inputs = (spectra, currents, land_mask, diffusion, courant, stokes_weight, stress_weight)
    kept, pay, ecol, wcol, local, coef = call(
        functools.partial(sums_kernel, z),
        (
            whole,
            flat(z.sec_tiles),
            flat(z.col_tiles),
            flat(z.col_tiles),
            flat(2),
            flat(z.coef_tiles),
        ),
        [ANY] * 7,
        scratch=[
            pltpu.VMEM(currents.shape, F32),
            pltpu.VMEM(land_mask.shape, jnp.int32),
            pltpu.SMEM(courant.shape, F32),
            pltpu.SMEM(courant.shape, F32),
            pltpu.SMEM(courant.shape, F32),
            pltpu.VMEM((5 * SUMS, ROWS, LANES), F32),
            sems,
            pltpu.SemaphoreType.DMA((6,)),
        ],
        name="spectra_sums",
        bytes_accessed=size,
        flops=16 * size // 4,
    )(*[pltpu.with_memory_space_constraint(array, pltpu.HBM) for array in inputs])

    other = shifted(pay, "sec", 1)

    got_first, got_second = [
        swapped(
            call(
                functools.partial(edge_rows_kernel, z, turn),
                (edge_rows,),
                [VMEM],
                name="pick_rows",
                bytes_accessed=size // 16,
                flops=2**16,
            )(kept)[0],
            turn,
        )
        for turn in range(2)
    ]

    (picks,) = call(
        functools.partial(picks_kernel, z),
        (jax.ShapeDtypeStruct((z.half * ROWS, LANES), BF16),),
        [VMEM],
        name="picks",
        bytes_accessed=size,
        flops=8388608,
    )(kept)

    fields, coup, flux, to_east, to_west = call(
        functools.partial(columns_kernel, z),
        (stack(z.fields), stack(4), flat(1 + z.sec_tiles - z.sec_rows), flat(1 + z.col_tiles), flat(1 + z.col_tiles)),
        [VMEM] * 6,
        name="pack_columns",
        bytes_accessed=2**18,
        flops=1073741824,
    )(pay, other, picks, local, ecol, wcol)

    from_east = shifted(to_west, "lon", -1)
    from_west = shifted(to_east, "lon", 1)

    coup, edges, to_first, to_second = call(
        functools.partial(rows_kernel, z),
        (stack(4), stack(z.arrays + SUMS), flat(z.lat_tiles), flat(z.lat_tiles)),
        [VMEM] * 7,
        name="pack_rows",
        bytes_accessed=2**18,
        flops=2**27,
    )(from_east, from_west, fields, coup, flux, local, got_second)

    from_second = swapped(to_second, 1)
    from_first = swapped(to_first, 0)

    new_spectra, coup = call(
        functools.partial(wave_kernel, z, lat_count),
        (jax.ShapeDtypeStruct(spectra.shape, F32), stack(4)),
        [VMEM] * 10,
        out_specs=[ANY, VMEM],
        scratch=[whole, pltpu.VMEM((directions, ROWS, LANES), F32), pltpu.VMEM((2, z.edge_rows, LANES), F32), sems],
        name="wave_step",
        bytes_accessed=2 * size,
        flops=9 * size // 4,
    )(kept, fields, coup, local, coef, picks, from_west, from_east, got_first, got_second)

    (new_currents,) = call(
        functools.partial(ocean_kernel, z, lat_count),
        (jax.ShapeDtypeStruct(currents.shape, F32),),
        [VMEM] * 7,
        scratch=[pltpu.VMEM((count, 2 * ROWS, 2 * LANES), F32) for count in (z.fields, z.fields, 2 * levels, 2 * levels)],
        name="ocean_steps",
        bytes_accessed=2**20,
        flops=2**20,
    )(from_first, from_second, fields, coup, flux, edges, local)
    return new_spectra, new_currents


def solution(mesh):
    in_specs = (
        P("sec", None, "lat", "lon"),
        P(None, "sec", "lat", "lon"),
        P("lat", "lon"),
        P("lat", "lon"),
        P("sec"),
        P("sec"),
        P("sec"),
    )
    out_specs = (P("sec", None, "lat", "lon"), P(None, "sec", "lat", "lon"))
    return jax.shard_map(shards, mesh=mesh, in_specs=in_specs, out_specs=out_specs, check_vma=False)
```

```python
import functools
import math

import jax
import jax.numpy as jnp
import numpy as np
from jax import lax
from jax.experimental import pallas as pl
from jax.experimental.pallas import tpu as pltpu
from jax.sharding import PartitionSpec as P

ITERS = 4
ROWS = 8
LANES = 128
HALO = 4
MOMENTS = 5
SUMS = 2 * MOMENTS
FLUX_COLS = 3
current_gain = 0.1
stress_gain = 0.5

VMEM = pl.BlockSpec(memory_space=pltpu.VMEM)
SMEM = pl.BlockSpec(memory_space=pltpu.SMEM)
ANY = pl.BlockSpec(memory_space=pl.ANY)
F32 = jnp.float32
BF16 = jnp.bfloat16


def lanes():
    return lax.broadcasted_iota(jnp.int32, (ROWS, LANES), 1)


def rows():
    return lax.broadcasted_iota(jnp.int32, (ROWS, LANES), 0)


def lane_roll(tile, shift):
    if isinstance(shift, int):
        shift %= LANES
        if shift == 0:
            return tile
    return pltpu.roll(tile, shift, 1)


def row_roll(tile, shift):
    shift %= ROWS
    return tile if shift == 0 else pltpu.roll(tile, shift, 0)


def spread(ref, row):
    return jnp.broadcast_to(ref[pl.ds(row, 1), :], (ROWS, LANES))


def put(ref, index, tile):
    ref[pl.ds(index * ROWS, ROWS), :] = tile


def take(ref, index):
    return ref[pl.ds(index * ROWS, ROWS), :]


def coupled(sums, zonal, meridional, sea):
    result = []
    for w in range(2):
        c, s, cc, cs, ss = sums[w * MOMENTS : (w + 1) * MOMENTS]
        result.append(sea * (c + current_gain * (zonal * cc + meridional * cs)))
        result.append(sea * (s + current_gain * (zonal * cs + meridional * ss)))
    return result


class Sizes:
    def __init__(self, freqs, directions, levels):
        self.freqs = freqs
        self.directions = directions
        self.levels = levels
        self.quarter = directions // 4
        self.fields = 2 * 2 * levels
        self.half = directions // 2
        self.per_tile = LANES // self.half
        self.col_tiles = -(-freqs // self.per_tile)
        self.edge_rows = -(-freqs * directions // 2 // ROWS) * ROWS
        assert self.half >= ROWS
        self.sec_sums = self.fields // 2
        self.sec_cols = self.sec_sums + SUMS
        self.sec_rows = self.sec_cols + 1
        self.sec_tiles = self.sec_rows + -(-2 * SUMS // ROWS)
        self.lon_coup = HALO * (self.fields + 2)
        self.lon_flux = self.lon_coup + 4 * HALO
        self.lon_rows = self.lon_flux + SUMS
        self.arrays = self.fields + 2 + 4
        self.pairs = self.arrays // 2
        self.flux_tiles = -(-SUMS // ROWS)
        self.lat_pairs = 0
        self.lat_flux = self.lat_pairs + self.pairs
        self.lat_edges = self.lat_flux + self.flux_tiles
        self.lat_tiles = self.lat_edges + 1
        self.coef_tiles = -(-freqs // ROWS)
        assert self.lon_rows + SUMS * FLUX_COLS <= LANES
        assert (self.pairs + self.flux_tiles) * 2 * HALO <= LANES

    def headings(self, i):
        q = self.quarter
        return (i, 2 * q - 1 - i, 2 * q + i, 4 * q - 1 - i)


def chunks(z):
    q = z.quarter
    cuts = sorted({0, q * 5 // 9, q})
    result = []
    for lo, hi in zip(cuts, cuts[1:]):
        starts = (lo, 2 * q - hi, 2 * q + lo, 4 * q - hi)
        result.append((lo, hi, [pl.ds(start, hi - lo) for start in starts]))
    return result


def sums_kernel(z, x, cur_in, mask_in, diffusion_in, courant_in, stokes_in, stress_in, buf, pay, ecol, wcol, local, coef, cur, mask, courant, stokes, stress, acc, sems, small_sems):
    q, nf = z.quarter, z.freqs
    pairs = ((cur_in, cur), (mask_in, mask), (diffusion_in, local.at[pl.ds(ROWS, ROWS)]), (courant_in, courant), (stokes_in, stokes), (stress_in, stress))
    small = [pltpu.make_async_copy(source, target, small_sems.at[k]) for k, (source, target) in enumerate(pairs)]
    copies = []
    for g, (_, _, spans) in enumerate(chunks(z)):
        for j, span in enumerate(spans):
            copies.append(pltpu.make_async_copy(x.at[:, span], buf.at[:, span], sems.at[4 * g + j]))
    for copy in copies + small:
        copy.start()

    lane, row = lanes(), rows()
    zero = jnp.zeros((ROWS, LANES), F32)
    for k in range(5 * SUMS):
        acc[k] = zero
    sizes = tables(z.directions)
    east, west = [zero] * z.col_tiles, [zero] * z.col_tiles
    for copy in small:
        copy.wait()
    sea = mask[...].astype(F32)
    put(local, 0, sea)
    for comp in range(2):
        for level in range(z.levels):
            put(pay, comp * z.levels + level, cur[comp, level] * sea)
    for t in range(z.coef_tiles):
        tile = zero
        for f in range(t * ROWS, min(nf, (t + 1) * ROWS)):
            tile = jnp.where(row == f - t * ROWS, courant[f], tile)
        put(coef, t, tile)

    def add(i):
        c, s = float(sizes[0, i]), float(sizes[1, i])
        heading = z.headings(i)
        total = [[zero] * 4 for _ in range(4)]
        for f in range(nf):
            t = f // z.per_tile
            cg = courant[f]
            factors = (stokes[f], stokes[f] * cg, stress[f], stress[f] * cg)
            for j in range(4):
                energy = buf[f, heading[j]]
                for k in range(4):
                    total[k][j] = total[k][j] + factors[k] * energy
                at = f % z.per_tile * z.half + 2 * i + (0 if j in (0, 1) else 1)
                if j in (0, 3):
                    east[t] = jnp.where(lane == at, lane_roll(energy, at - (LANES - 1)), east[t])
                else:
                    west[t] = jnp.where(lane == at, lane_roll(energy, at), west[t])
        cc, cs, ss = c * c, c * s, s * s
        for w in range(2):
            plain, fast = total[2 * w], total[2 * w + 1]
            both = c + s
            h = [plain[j] - both * fast[j] for j in range(4)]
            here, there = h[0] + h[3], h[1] + h[2]
            every = here + there
            values = [
                c * (here - there),
                s * ((h[0] + h[1]) - (h[2] + h[3])),
                cc * every,
                cs * ((h[0] - h[3]) + (h[2] - h[1])),
                ss * every,
            ]
            for a, b, size, signs in (
                (fast[0] + fast[3], fast[0] - fast[3], c, (1, 1, 1)),
                (fast[1] + fast[2], fast[1] - fast[2], c, (-1, 1, -1)),
            ):
                values += [signs[0] * size * c * a, signs[1] * size * s * b, size * cc * a, signs[2] * size * cs * b, size * ss * a]
            for a, b, size, signs in (
                (fast[0] + fast[1], fast[0] - fast[1], s, (1, 1, 1)),
                (fast[2] + fast[3], fast[3] - fast[2], s, (1, -1, -1)),
            ):
                values += [signs[0] * size * c * b, signs[1] * size * s * a, size * cc * a, signs[2] * size * cs * b, size * ss * a]
            for kind in range(5):
                for m in range(MOMENTS):
                    at = kind * SUMS + w * MOMENTS + m
                    acc[at] = acc[at] + values[kind * MOMENTS + m]

    for g, (lo, hi, _) in enumerate(chunks(z)):
        for copy in copies[4 * g : 4 * g + 4]:
            copy.wait()
        for i in range(lo, hi):
            add(i)
    for t in range(z.col_tiles):
        put(ecol, t, east[t])
        put(wcol, t, west[t])

    cols = zero
    rims = [zero] * (z.sec_tiles - z.sec_rows)
    for k in range(SUMS):
        center, east, west, north, south = (acc[kind * SUMS + k] for kind in range(5))
        value = center + jnp.where(lane > 0, lane_roll(east, 1), 0.0) + jnp.where(lane < LANES - 1, lane_roll(west, -1), 0.0)
        value = value + jnp.where(row > 0, row_roll(north, 1), 0.0) + jnp.where(row < ROWS - 1, row_roll(south, -1), 0.0)
        put(pay, z.sec_sums + k, value)
        cols = jnp.where(lane == k, lane_roll(east, k - (LANES - 1)), cols)
        cols = jnp.where(lane == SUMS + k, lane_roll(west, SUMS + k), cols)
        for at, tile, edge in ((k, north, ROWS - 1), (SUMS + k, south, 0)):
            t, r = at // ROWS, at % ROWS
            rims[t] = jnp.where(row == r, row_roll(tile, r - edge), rims[t])
    put(pay, z.sec_cols, cols)
    for t, tile in enumerate(rims):
        put(pay, z.sec_rows + t, tile)


def parts(tile):
    high = tile.astype(BF16).astype(F32)
    return high, (tile - high).astype(BF16).astype(F32)


def edge_rows_kernel(z, turn, x, out):
    flat = x.reshape(z.freqs * z.directions * ROWS, LANES)
    north, south = ROWS - 1, z.half * ROWS
    start = jnp.where(lax.rem(lax.axis_index("lat"), 2) == turn, north, south)
    out[pl.ds(z.edge_rows - ROWS, ROWS), :] = jnp.zeros((ROWS, LANES), F32)
    for f in range(z.freqs):
        for first in [*range(0, z.half - ROWS, ROWS), z.half - ROWS]:
            eight = flat[pl.ds((f * z.directions + first) * ROWS + start, ROWS, stride=ROWS), :]
            out[pl.ds(f * z.half + first, ROWS), :] = eight


def picks_kernel(z, x, picks):
    lane = lanes()
    for k in range(z.half // 2):
        both = [((lane & (LANES // 2 - 1)) == 2 * k + n).astype(F32) for n in range(2)]
        picks[pl.ds(2 * ROWS * k, 2 * ROWS), :] = jnp.concatenate(both, axis=0).astype(BF16)


def columns_kernel(z, mine, other, picks, local, ecol, wcol, fields, coup, flux, to_east, to_west):
    lane, row = lanes(), rows()
    sec = lax.axis_index("sec")
    total = 2 * z.levels
    for comp in range(2):
        for level in range(z.levels):
            own = level + sec * (z.levels - 1 - 2 * level)
            far = z.levels + level + sec * (z.levels - 1 - 2 * level)
            fields[comp * total + own] = take(mine, comp * z.levels + level)
            fields[comp * total + far] = take(other, comp * z.levels + level)
    sea, diffusion = take(local, 0), take(local, 1)
    top = sec * (total - 1)
    zonal, meridional = fields[top], fields[total + top]
    sums = [take(mine, z.sec_sums + k) + take(other, z.sec_sums + k) for k in range(SUMS)]
    coupling = coupled(sums, zonal, meridional, sea)
    cols = take(mine, z.sec_cols) + take(other, z.sec_cols)
    put(flux, 0, cols)
    for t in range(z.sec_tiles - z.sec_rows):
        put(flux, 1 + t, take(mine, z.sec_rows + t) + take(other, z.sec_rows + t))
    for k in range(4):
        coup[k] = coupling[k]
    arrays = [fields[k] for k in range(z.fields)] + [sea, diffusion] + coupling
    east, west = lane_roll(cols, z.lon_flux), lane_roll(cols, z.lon_flux - SUMS)
    for k, array in enumerate(arrays):
        mine_here = (lane >= HALO * k) & (lane < HALO * (k + 1))
        east = jnp.where(mine_here, lane_roll(array, HALO * (k + 1)), east)
        west = jnp.where(mine_here, lane_roll(array, HALO * k), west)
    for k in range(SUMS):
        edge = jnp.where(row == ROWS - 1, spread(flux, ROWS + k), spread(flux, ROWS + SUMS + k))
        at = z.lon_rows + FLUX_COLS * k
        mine_here = (lane >= at) & (lane < at + FLUX_COLS)
        east = jnp.where(mine_here, lane_roll(edge, at + FLUX_COLS), east)
        west = jnp.where(mine_here, lane_roll(edge, at), west)
    put(to_east, 0, east)
    put(to_west, 0, west)
    for t in range(z.col_tiles):
        put(to_east, 1 + t, take(ecol, t))
        put(to_west, 1 + t, take(wcol, t))


def rows_kernel(z, from_east, from_west, fields, coup, flux, local, got_rows, coup_out, edges, to_first, to_second):
    lane, row = lanes(), rows()
    total = 2 * z.levels
    top = lax.axis_index("sec") * (total - 1)
    sea, diffusion = take(local, 0), take(local, 1)
    cols = take(flux, 0)
    west, east = take(from_west, 0), take(from_east, 0)

    def beyond(first, width):
        near = lane_roll(east, -first)
        far = lane_roll(west, LANES - width - first)
        return jnp.where(lane < width, near, jnp.where(lane >= LANES - width, far, 0.0))

    edge = [beyond(HALO * k, HALO) for k in range(z.fields + 2)]
    for k in range(z.fields + 2):
        edges[k] = edge[k]
    inner, outer = [], []
    for k in range(SUMS):
        at = z.lon_flux + k
        inner.append(jnp.where(lane == 0, lane_roll(west, -at), jnp.where(lane == LANES - 1, lane_roll(east, LANES - 1 - at), 0.0)))
        outer.append(jnp.where(lane == 0, lane_roll(cols, -k), jnp.where(lane == LANES - 1, lane_roll(cols, LANES - 1 - SUMS - k), 0.0)))
    inside = coupled(inner, fields[top], fields[total + top], sea)
    outside = coupled(outer, edges[top], edges[total + top], edge[z.fields])
    main_coupling = [coup[k] + inside[k] for k in range(4)]
    edge_coupling = [beyond(z.lon_coup + HALO * k, HALO) + outside[k] for k in range(4)]
    for k in range(4):
        coup_out[k] = main_coupling[k]
        edges[z.fields + 2 + k] = edge_coupling[k]
    row_edge = [beyond(z.lon_rows + FLUX_COLS * k, FLUX_COLS) for k in range(SUMS)]
    for k in range(SUMS):
        edges[z.arrays + k] = row_edge[k]

    main = [fields[k] for k in range(z.fields)] + [sea, diffusion] + main_coupling
    edge = edge + edge_coupling
    low = row < HALO
    odd = lax.rem(lax.axis_index("lat"), 2) == 1

    def send(index, north, south):
        put(to_first, index, jnp.where(odd, south, north))
        put(to_second, index, jnp.where(odd, north, south))

    def pair(a, b):
        return jnp.where(low, row_roll(b, HALO), a), jnp.where(low, a, row_roll(b, HALO))

    def group(tile, k):
        at = 2 * HALO * k
        in_group = lax.rem(lane + LANES + HALO - at, LANES) < 2 * HALO
        return in_group, lane_roll(tile, at)

    north_edges = jnp.zeros((ROWS, LANES), F32)
    south_edges = north_edges
    for k in range(z.pairs):
        north, south = pair(main[2 * k], main[2 * k + 1])
        send(z.lat_pairs + k, north, south)
        north, south = pair(edge[2 * k], edge[2 * k + 1])
        in_group, moved = group(north, k)
        north_edges = jnp.where(in_group, moved, north_edges)
        in_group, moved = group(south, k)
        south_edges = jnp.where(in_group, moved, south_edges)
    for t in range(z.flux_tiles):
        north, south = jnp.zeros((ROWS, LANES), F32), jnp.zeros((ROWS, LANES), F32)
        north_row, south_row = north, south
        for r in range(min(ROWS, SUMS - t * ROWS)):
            k = t * ROWS + r
            north = jnp.where(row == r, spread(flux, ROWS + k), north)
            south = jnp.where(row == r, spread(flux, ROWS + SUMS + k), south)
            north_row = jnp.where(row == r, jnp.broadcast_to(row_edge[k][ROWS - 1 :], (ROWS, LANES)), north_row)
            south_row = jnp.where(row == r, jnp.broadcast_to(row_edge[k][:1], (ROWS, LANES)), south_row)
        send(z.lat_flux + t, north, south)
        in_group, moved = group(north_row, z.pairs + t)
        north_edges = jnp.where(in_group, moved, north_edges)
        in_group, moved = group(south_row, z.pairs + t)
        south_edges = jnp.where(in_group, moved, south_edges)
    send(z.lat_edges, north_edges, south_edges)


def side_signs(j):
    return (1 if j in (0, 3) else -1), (1 if j in (0, 1) else -1)


def lat_sides(first, second, lat_count):
    place = lax.axis_index("lat")
    odd = lax.rem(place, 2) == 1
    north = jnp.where(place < lat_count - 1, jnp.where(odd, second, first), 0.0)
    south = jnp.where(place > 0, jnp.where(odd, first, second), 0.0)
    return north, south


def wave_kernel(z, lat_count, x, fields, coup, local, coef, picks, from_west, from_east, first, second, out, coup_out, buf, scales, sides, sems):
    q, nf, half = z.quarter, z.freqs, z.half
    lane, row = lanes(), rows()
    total = 2 * z.levels
    top = lax.axis_index("sec") * (total - 1)
    sea = take(local, 0)
    zonal, meridional = current_gain * fields[top], current_gain * fields[total + top]
    coup_out[...] = coup[...]
    place = lax.axis_index("lat")
    odd = lax.rem(place, 2)
    sides[odd] = jnp.where((odd == 1) | (place < lat_count - 1), first[...], 0.0)
    sides[1 - odd] = jnp.where((place > 0) & ((odd == 0) | (place < lat_count - 1)), second[...], 0.0)
    sizes = tables(z.directions)
    headings = []
    for i in range(q):
        c, s = float(sizes[0, i]), float(sizes[1, i])
        for j, heading in enumerate(z.headings(i)):
            sign_x, sign_y = side_signs(j)
            headings.append((heading, i, sign_x, sign_y, 2 * i + (0 if j in (0, 1) else 1)))
            scales[heading] = sea * (1.0 + (sign_x * c) * zonal + (sign_y * s) * meridional)
    ones = jnp.ones((LANES, LANES), BF16)

    def body(f, _):
        speed = spread(coef, f)
        along = [speed * float(sizes[0, i]) for i in range(q)]
        across = [speed * float(sizes[1, i]) for i in range(q)]
        stay = [1.0 - along[i] - across[i] for i in range(q)]
        at = pl.ds(pl.multiple_of((1 + (f // z.per_tile)) * ROWS, ROWS), ROWS)
        back = LANES - half * (f % z.per_tile)
        rims = []
        for ref in (from_west, from_east):
            high, low = parts(lane_roll(ref[at, :], back))
            both = jnp.where(lane < LANES // 2, high, lane_roll(low, LANES // 2))
            both = jnp.concatenate([both, both], axis=0).astype(BF16)
            chosen = jnp.concatenate([both] * (half // 2), axis=0) * picks[...]
            rims.append(jnp.dot(chosen, ones, preferred_element_type=F32))
        for heading, i, sign_x, sign_y, k in headings:
            energy = x[f, heading]
            if sign_x > 0:
                beside = jnp.where(lane == 0, rims[0][k * ROWS : (k + 1) * ROWS], lane_roll(energy, 1))
            else:
                beside = jnp.where(lane == LANES - 1, rims[1][k * ROWS : (k + 1) * ROWS], lane_roll(energy, -1))
            if sign_y > 0:
                below = jnp.where(row == 0, spread(sides.at[1], f * half + heading), row_roll(energy, 1))
            else:
                below = jnp.where(row == ROWS - 1, spread(sides.at[0], f * half + heading - half), row_roll(energy, -1))
            buf[f, heading] = scales[heading] * (stay[i] * energy + along[i] * beside + across[i] * below)
        return 0

    count = 6 if nf % 6 == 0 else 1
    copies = []
    for g in range(count):
        span = pl.ds(g * (nf // count), nf // count)
        lax.fori_loop(g * (nf // count), (g + 1) * (nf // count), body, 0, unroll=3 if nf % 18 == 0 else 1)
        copy = pltpu.make_async_copy(buf.at[span], out.at[span], sems.at[g])
        copy.start()
        copies.append(copy)
    for copy in copies:
        copy.wait()


def ocean_kernel(z, lat_count, from_first, from_second, fields, coup, flux, edges, local, currents_out, ext, force, still, mixed):
    total = 2 * z.levels
    row = rows()
    sec = lax.axis_index("sec")
    sea, diffusion = take(local, 0), take(local, 1)
    low = row < HALO

    def pair(north, south):
        first = jnp.where(low, north, south)
        second = jnp.where(low, row_roll(north, HALO), row_roll(south, HALO))
        return first, second

    def sides(index):
        return lat_sides(take(from_first, index), take(from_second, index), lat_count)

    north_edges, south_edges = sides(z.lat_edges)
    north_rows, south_rows = zip(*[sides(z.lat_flux + t) for t in range(z.flux_tiles)])
    halo, halo_edge = [], []
    for k in range(z.pairs):
        halo += pair(*sides(z.lat_pairs + k))
        halo_edge += [lane_roll(tile, -2 * HALO * k) for tile in pair(north_edges, south_edges)]
    inner, outer, inner_edge, outer_edge = [], [], [], []
    edge_rows = [[lane_roll(tile, -2 * HALO * (z.pairs + t)) for tile in (north_edges, south_edges)] for t in range(z.flux_tiles)]
    for k in range(SUMS):
        t, r = k // ROWS, k % ROWS
        high = row == ROWS - 1
        bottom = row == 0
        north = jnp.broadcast_to(north_rows[t][r : r + 1], (ROWS, LANES))
        south = jnp.broadcast_to(south_rows[t][r : r + 1], (ROWS, LANES))
        inner.append(jnp.where(high, north, jnp.where(bottom, south, 0.0)))
        outer.append(jnp.where(bottom, spread(flux, ROWS + k), jnp.where(high, spread(flux, ROWS + SUMS + k), 0.0)))
        north, south = [jnp.broadcast_to(tile[r : r + 1], (ROWS, LANES)) for tile in edge_rows[t]]
        inner_edge.append(jnp.where(high, north, jnp.where(bottom, south, 0.0)))
        mine = edges[z.arrays + k]
        outer_edge.append(
            jnp.where(bottom, jnp.broadcast_to(mine[ROWS - 1 :], (ROWS, LANES)), jnp.where(high, jnp.broadcast_to(mine[:1], (ROWS, LANES)), 0.0))
        )

    def joined(main, edge, halo_main, halo_side):
        return jnp.concatenate([jnp.concatenate([main, edge], axis=1), jnp.concatenate([halo_main, halo_side], axis=1)], axis=0)

    whole = [joined(fields[k], edges[k], halo[k], halo_edge[k]) for k in range(z.fields)]
    for k in range(z.fields):
        ext[k] = whole[k]
    zonal, meridional = [jnp.where(sec == 0, whole[comp * total], whole[comp * total + total - 1]) for comp in range(2)]
    sea_all = joined(sea, edges[z.fields], halo[z.fields], halo_edge[z.fields])
    kappa = joined(diffusion, edges[z.fields + 1], halo[z.fields + 1], halo_edge[z.fields + 1])
    sums = [joined(inner[k], inner_edge[k], outer[k], outer_edge[k]) for k in range(SUMS)]
    extra = coupled(sums, zonal, meridional, sea_all)
    first = z.fields + 2
    coupling = [joined(coup[k], edges[first + k], halo[first + k], halo_edge[first + k]) + extra[k] for k in range(4)]

    shape = (2 * ROWS, 2 * LANES)
    row_all = lax.broadcasted_iota(jnp.int32, shape, 0)
    row_all = jnp.where(row_all >= 2 * ROWS - HALO, row_all - 2 * ROWS, row_all) + lax.axis_index("lat") * ROWS
    rot = sea_all * (0.05 + 0.1 * (row_all.astype(F32) + 0.5) * (1.0 / (lat_count * ROWS)))
    spin = sea_all * kappa

    def by_level(function, p):
        return jnp.where(sec == 0, function(p), function(total - 1 - p)).astype(F32)

    for p in range(total):
        mix, decay, gain = by_level(lambda level: 0.04 + 0.0125 * (7 * level % 5), p), by_level(lambda level: 1.0 / (1.0 + level), p), by_level(lambda level: stress_gain if level == 0 else 0.0, p)
        force[p] = rot * decay * coupling[1] + sea_all * gain * coupling[2]
        force[total + p] = sea_all * gain * coupling[3] - rot * decay * coupling[0]
        mixed[p] = sea_all * mix
        still[p] = sea_all * (1.0 - mix * (1 if p in (0, total - 1) else 2)) - 4.0 * spin
    for step in range(ITERS):
        needed = min(total, z.levels + ITERS - 1 - step)
        every = [ext[comp * total + p] for comp in range(2) for p in range(needed)]
        after = []
        for comp in range(2):
            for p in range(needed):
                at = comp * needed + p
                value = every[at]
                around = (pltpu.roll(value, 1, 1) + pltpu.roll(value, 2 * LANES - 1, 1)) + (pltpu.roll(value, 1, 0) + pltpu.roll(value, 2 * ROWS - 1, 0))
                near = [ext[comp * total + other] for other in (p - 1, p + 1) if 0 <= other < total]
                turned = rot * ext[(1 - comp) * total + p]
                moved = still[p] * value + spin * around + mixed[p] * sum(near[1:], near[0]) + force[comp * total + p]
                after.append(moved + turned if comp == 0 else moved - turned)
        if step < ITERS - 1:
            for comp in range(2):
                for p in range(needed):
                    ext[comp * total + p] = after[comp * needed + p]
        else:
            for comp in range(2):
                for level in range(z.levels):
                    place = level + sec * (z.levels - 1 - 2 * level)
                    currents_out[comp, place] = after[comp * needed + level][:ROWS, :LANES]


def tables(directions):
    quarter = directions // 4
    heading = (np.arange(quarter) + 0.5) * (2.0 * math.pi / directions)
    return np.stack([np.cos(heading), np.sin(heading)]).astype(np.float32)


def shifted(value, axis, steps):
    count = lax.axis_size(axis)
    return lax.ppermute(value, axis, [(i, (i + steps) % count) for i in range(count)])


def swapped(value, parity):
    lat, lon = lax.axis_size("lat"), lax.axis_size("lon")
    pairs = []
    for i in range(lat):
        other = i + 1 if i % 2 == parity else i - 1
        for j in range(lon):
            if 0 <= other < lat:
                pairs.append((i * lon + j, other * lon + j))
            elif j ^ 1 < lon:
                pairs.append((i * lon + j, i * lon + (j ^ 1)))
    return lax.ppermute(value, ("lat", "lon"), pairs)


def flat(tiles):
    return jax.ShapeDtypeStruct((tiles * ROWS, LANES), F32)


def stack(count):
    return jax.ShapeDtypeStruct((count, ROWS, LANES), F32)


def call(kernel, out_shape, in_specs, out_specs=None, scratch=(), name=None, bytes_accessed=0, flops=0):
    return pl.pallas_call(
        kernel,
        out_shape=out_shape,
        in_specs=in_specs,
        out_specs=out_specs if out_specs is not None else [VMEM] * len(out_shape),
        scratch_shapes=list(scratch),
        name=name,
        compiler_params=pltpu.CompilerParams(vmem_limit_bytes=24 * 1024 * 1024),
        cost_estimate=pl.CostEstimate(flops=flops, bytes_accessed=bytes_accessed, transcendentals=0),
    )


def shards(spectra, currents, land_mask, diffusion, courant, stokes_weight, stress_weight):
    freqs, directions, tile_rows, tile_cols = spectra.shape
    levels = currents.shape[1]
    lat_count = lax.axis_size("lat")
    assert lax.axis_size("sec") == 2 and (tile_rows, tile_cols) == (ROWS, LANES) and directions % 4 == 0
    z = Sizes(freqs, directions, levels)
    size = spectra.size * 4
    copies = 4 * len(chunks(z))
    sems = pltpu.SemaphoreType.DMA((copies,))
    whole = pltpu.VMEM(spectra.shape, F32)

    edge_rows = jax.ShapeDtypeStruct((z.edge_rows, LANES), F32)
    inputs = (spectra, currents, land_mask, diffusion, courant, stokes_weight, stress_weight)
    kept, pay, ecol, wcol, local, coef = call(
        functools.partial(sums_kernel, z),
        (
            whole,
            flat(z.sec_tiles),
            flat(z.col_tiles),
            flat(z.col_tiles),
            flat(2),
            flat(z.coef_tiles),
        ),
        [ANY] * 7,
        scratch=[
            pltpu.VMEM(currents.shape, F32),
            pltpu.VMEM(land_mask.shape, jnp.int32),
            pltpu.SMEM(courant.shape, F32),
            pltpu.SMEM(courant.shape, F32),
            pltpu.SMEM(courant.shape, F32),
            pltpu.VMEM((5 * SUMS, ROWS, LANES), F32),
            sems,
            pltpu.SemaphoreType.DMA((6,)),
        ],
        name="spectra_sums",
        bytes_accessed=size,
        flops=16 * size // 4,
    )(*[pltpu.with_memory_space_constraint(array, pltpu.HBM) for array in inputs])

    other = shifted(pay, "sec", 1)

    got_first, got_second = [
        swapped(
            call(
                functools.partial(edge_rows_kernel, z, turn),
                (edge_rows,),
                [VMEM],
                name="pick_rows",
                bytes_accessed=size // 16,
                flops=2**16,
            )(kept)[0],
            turn,
        )
        for turn in range(2)
    ]

    (picks,) = call(
        functools.partial(picks_kernel, z),
        (jax.ShapeDtypeStruct((z.half * ROWS, LANES), BF16),),
        [VMEM],
        name="picks",
        bytes_accessed=size,
        flops=8388608,
    )(kept)

    fields, coup, flux, to_east, to_west = call(
        functools.partial(columns_kernel, z),
        (stack(z.fields), stack(4), flat(1 + z.sec_tiles - z.sec_rows), flat(1 + z.col_tiles), flat(1 + z.col_tiles)),
        [VMEM] * 6,
        name="pack_columns",
        bytes_accessed=2**18,
        flops=1073741824,
    )(pay, other, picks, local, ecol, wcol)

    from_east = shifted(to_west, "lon", -1)
    from_west = shifted(to_east, "lon", 1)

    coup, edges, to_first, to_second = call(
        functools.partial(rows_kernel, z),
        (stack(4), stack(z.arrays + SUMS), flat(z.lat_tiles), flat(z.lat_tiles)),
        [VMEM] * 7,
        name="pack_rows",
        bytes_accessed=2**18,
        flops=2**27,
    )(from_east, from_west, fields, coup, flux, local, got_second)

    from_second = swapped(to_second, 1)
    from_first = swapped(to_first, 0)

    new_spectra, coup = call(
        functools.partial(wave_kernel, z, lat_count),
        (jax.ShapeDtypeStruct(spectra.shape, F32), stack(4)),
        [VMEM] * 10,
        out_specs=[ANY, VMEM],
        scratch=[whole, pltpu.VMEM((directions, ROWS, LANES), F32), pltpu.VMEM((2, z.edge_rows, LANES), F32), sems],
        name="wave_step",
        bytes_accessed=2 * size,
        flops=9 * size // 4,
    )(kept, fields, coup, local, coef, picks, from_west, from_east, got_first, got_second)

    (new_currents,) = call(
        functools.partial(ocean_kernel, z, lat_count),
        (jax.ShapeDtypeStruct(currents.shape, F32),),
        [VMEM] * 7,
        scratch=[pltpu.VMEM((count, 2 * ROWS, 2 * LANES), F32) for count in (z.fields, z.fields, 2 * levels, 2 * levels)],
        name="ocean_steps",
        bytes_accessed=2**20,
        flops=2**20,
    )(from_first, from_second, fields, coup, flux, edges, local)
    return new_spectra, new_currents


def solution(mesh):
    in_specs = (
        P("sec", None, "lat", "lon"),
        P(None, "sec", "lat", "lon"),
        P("lat", "lon"),
        P("lat", "lon"),
        P("sec"),
        P("sec"),
        P("sec"),
    )
    out_specs = (P("sec", None, "lat", "lon"), P(None, "sec", "lat", "lon"))
    return jax.shard_map(shards, mesh=mesh, in_specs=in_specs, out_specs=out_specs, check_vma=False)
```
